256 devices in a mesh: src: 16 (over z, core), tgt: 16 (over y, x).
Axes of the slice: x: 4, y: 4, z: 8, core: 2. Of those that a mesh axis runs over, the one named last changes fastest.
Arguments:
- source_latent: float32 [32768, 32], P(('src', 'tgt')), may hold values from -1.5 to 1.5
- source_left: float32 [32768, 34], P(('src', 'tgt')), may hold values from -1 to 1
- source_right: float32 [32768, 34], P(('src', 'tgt')), may hold values from 0.1 to 1.9
- source_logw: float32 [32768], P(('src', 'tgt')), as said below
- target_latent: float32 [16, 16, 128, 32], P('tgt', 'src'), may hold values from -1.5 to 1.5
- target_left: float32 [16, 16, 128, 34], P('tgt', 'src'), may hold values from -1 to 1
- target_right: float32 [16, 16, 128, 34], P('tgt', 'src'), may hold values from 0.1 to 1.9
- target_logw: float32 [16, 16, 128], P('tgt', 'src'), as said below
- target_potential: float32 [16, 16, 128], P('tgt', 'src'), may hold values from -0.6 to 36
- old_moment: float32 [34, 34], replicated, may hold values from 0.05 to 0.5
Outputs:
- source_potential: float32 [32768], P('src')
- new_potential: float32 [32768], P('tgt')
The draws below stay inside these ranges and needn't reach their ends.
Inputs may be any that keep to these rules, and one draw needn't show every extreme that they name: `source_logw`: log weights of the source cells, exp of which sums to about one. `target_logw`: log weights of the target cells, exp of which sums to about one.
All inputs are finite; a program needn't handle non-finite values.
Results may differ from the reference program's by a relative error of at most 0.0003.
Values sent between devices are 32-bit elements; how exact they have to be, the bound alone decides.
No kernel may reach another device: no remote copies, remote signals or barrier semaphores. Data moves between devices by JAX's collectives and lax.ppermute only.
A program may use at most 64 MiB of HBM per device.

```python
import jax
import jax.numpy as jnp
from jax import lax

LATENT = 32
RANK = 34
ITERS = 2
TILE = 2048
NCELLS = 32768
COL_BLOCK = 2048
N_SRC = 16
N_TGT = 16


def ramped_logw(key, shape, climb, spread):
    count = 1
    for extent in shape:
        count = count * extent
    position = jnp.arange(count, dtype=jnp.float32).reshape(shape) / float(max(count - 1, 1))
    noise = jax.random.uniform(key, shape, jnp.float32, -spread, spread)
    return -jnp.log(float(count)) + jnp.log(1.0 + climb * position) - jnp.log(1.0 + 0.5 * climb) + noise


def latent_field(key, stream_salt, shape, normal_part):
    first = jax.random.fold_in(jax.random.fold_in(key, stream_salt), 0)
    values = normal_part * jax.random.normal(first, shape, jnp.float32)
    return jnp.clip(values, -1.5, 1.5)


def spread_factor(key, latent, normal_part):
    first = jax.random.fold_in(key, 0)
    shape = latent.shape[:-1] + (RANK,)
    noise = normal_part * jax.random.normal(first, shape, jnp.float32)
    picked = jnp.take(latent, jnp.arange(RANK) % LATENT, axis=-1)
    return jnp.clip(1.0 + 2.0 * picked + noise, 0.1, 1.9)


def offset_factor(key, row_shape, center_value, row_swing, normal_part):
    first, second = jax.random.split(key, 2)
    offset = center_value + row_swing * jax.random.uniform(first, row_shape + (1,), jnp.float32, -1.0, 1.0)
    shape = row_shape + (RANK,)
    noise = normal_part * jax.random.normal(second, shape, jnp.float32)
    return jnp.clip(offset + noise, -1.0, 1.0)


def draw_source_latent(key, part):
    return latent_field(key, 101, (NCELLS, LATENT), 0.25)


def draw_target_latent(key, part):
    shape = (N_TGT, N_SRC, COL_BLOCK // N_SRC, LATENT)
    return latent_field(key, 103, shape, 0.25)


def draw_source_right(key, part):
    latent = latent_field(key, 101, (NCELLS, LATENT), 0.25)
    return spread_factor(jax.random.fold_in(key, 23), latent, 0.1)


def draw_target_right(key, part):
    shape = (N_TGT, N_SRC, COL_BLOCK // N_SRC, LATENT)
    latent = latent_field(key, 103, shape, 0.25)
    return spread_factor(jax.random.fold_in(key, 27), latent, 0.1)


def draw_source_left(key, part):
    key = jax.random.fold_in(key, 29)
    return offset_factor(key, (NCELLS,), 0.0, 0.25, 0.1715)


def draw_target_left(key, part):
    key = jax.random.fold_in(key, 31)
    row_shape = (N_TGT, N_SRC, COL_BLOCK // N_SRC)
    return offset_factor(key, row_shape, 0.1, 0.03, 0.1715)


def draw_source_logw(key, part):
    key = jax.random.fold_in(key, 11)
    return ramped_logw(key, (NCELLS,), 4.0, 0.5)


def draw_target_logw(key, part):
    key = jax.random.fold_in(key, 13)
    shape = (N_TGT, N_SRC, COL_BLOCK // N_SRC)
    return ramped_logw(key, shape, 4.0, 0.5)


def draw_target_potential(key, part):
    key = jax.random.fold_in(key, 7)
    shape = (N_TGT, N_SRC, COL_BLOCK // N_SRC)
    first = jax.random.fold_in(key, 0)
    return jnp.clip(0.1 * jax.random.normal(first, shape, jnp.float32), -0.6, 0.6)


def setup_inputs(seed: int = 0) -> dict:
    key_of = jax.random.split(jax.random.key(seed), 11)
    return {
        "source_latent": draw_source_latent(jax.random.fold_in(key_of[10], 71), 0),
        "source_left": draw_source_left(jax.random.fold_in(key_of[10], 71), 0),
        "source_right": draw_source_right(jax.random.fold_in(key_of[10], 71), 0),
        "source_logw": draw_source_logw(jax.random.fold_in(key_of[10], 71), 0),
        "target_latent": draw_target_latent(jax.random.fold_in(key_of[10], 71), 0),
        "target_left": draw_target_left(jax.random.fold_in(key_of[10], 71), 0),
        "target_right": draw_target_right(jax.random.fold_in(key_of[10], 71), 0),
        "target_logw": draw_target_logw(jax.random.fold_in(key_of[10], 71), 0),
        "target_potential": draw_target_potential(jax.random.fold_in(key_of[10], 71), 0),
        "old_moment": jnp.clip(jax.random.uniform(key_of[9], (RANK, RANK), jnp.float32, 0.05, 0.5), 0.05, 0.5),
    }


entropy_weight = 0.1
joining_weight = 0.5


def build_cost(u, v, a1, a2, moment, row_sq, col_sq):
    left = jnp.concatenate([u * (-2.0 * (1.0 - joining_weight)), jnp.dot(a1, moment, precision=lax.Precision.HIGHEST, preferred_element_type=jnp.float32) * (-2.0 * joining_weight)], axis=1)
    right = jnp.concatenate([v, a2], axis=1)
    cross = lax.dot_general(left, right, (((1,), (1,)), ((), ())), precision=lax.Precision.HIGHEST, preferred_element_type=jnp.float32)
    return cross + (1.0 - joining_weight) * (row_sq[:, None] + col_sq[None, :])


def reference(source_latent, source_left, source_right, source_logw, target_latent, target_left, target_right, target_logw, target_potential, old_moment):
    u, a1, b1, la = source_latent, source_left, source_right, source_logw
    v = target_latent.reshape(-1, LATENT)
    a2 = target_left.reshape(-1, RANK)
    b2 = target_right.reshape(-1, RANK)
    lb = target_logw.reshape(-1)
    g = target_potential.reshape(-1)
    row_sq = jnp.sum(u * u, axis=1)
    col_sq = jnp.sum(v * v, axis=1)
    blocks = NCELLS // TILE
    indices = jnp.arange(blocks, dtype=jnp.int32)

    def rows_of(x, k):
        return lax.dynamic_slice_in_dim(x, (k * TILE).astype(jnp.int32), TILE, 0)

    def cost_rows(k, moment):
        return build_cost(rows_of(u, k), v, rows_of(a1, k), a2, moment, rows_of(row_sq, k), col_sq)

    def f_update(gvec, moment):
        def one(k):
            c = cost_rows(k, moment)
            return entropy_weight * rows_of(la, k) - entropy_weight * jax.nn.logsumexp((gvec[None, :] - c) / entropy_weight, axis=1)
        return lax.map(one, indices).reshape(-1)

    def g_update(fvec, moment):
        def step(carry, k):
            top, total = carry
            scores = (rows_of(fvec, k)[:, None] - cost_rows(k, moment)) / entropy_weight
            upper = jnp.maximum(top, jnp.max(scores, axis=0))
            total = total * jnp.exp(top - upper) + jnp.sum(jnp.exp(scores - upper[None, :]), axis=0)
            return (upper, total), None
        init = (jnp.full((NCELLS,), -jnp.inf, jnp.float32), jnp.zeros((NCELLS,), jnp.float32))
        (top, total), _ = lax.scan(step, init, indices)
        return entropy_weight * lb - entropy_weight * (top + jnp.log(total))

    f = f_update(g, old_moment)

    def add_moment(acc, k):
        c = cost_rows(k, old_moment)
        plan = jnp.exp((rows_of(f, k)[:, None] + g[None, :] - c) / entropy_weight)
        carried = jnp.dot(plan, b2, precision=lax.Precision.HIGHEST, preferred_element_type=jnp.float32)
        term = lax.dot_general(rows_of(b1, k), carried, (((0,), (0,)), ((), ())), precision=lax.Precision.HIGHEST, preferred_element_type=jnp.float32)
        return acc + term, None

    moment, _ = lax.scan(add_moment, jnp.zeros((RANK, RANK), jnp.float32), indices)
    for step_index in range(ITERS):
        g = g_update(f, moment)
        f = f_update(g, moment)
    return f, g
```

```python
import functools

import jax
import jax.numpy as jnp
from jax import lax
from jax.experimental import pallas as pl
from jax.experimental.pallas import tpu as pltpu
from jax.sharding import PartitionSpec as P

LATENT = 32
RANK = 34
FEAT = 80
BIAS = 3 * FEAT
DEPTH = 256
LANES = 128
ENTROPY = 0.1
LOG2E = 1.4426950408889634
SCALE = LOG2E / ENTROPY

ROW_LOGW = LATENT + RANK
ROW_POT = ROW_LOGW + 1
ROW_RIGHT = 72
PACK = 112

f32 = jnp.float32
bf16 = jnp.bfloat16


def dot(a, b):
    return jnp.dot(a, b, preferred_element_type=f32)


def dot_nt(a, b):
    return lax.dot_general(a, b, (((1,), (1,)), ((), ())), preferred_element_type=f32)


def split(x):
    hi = x.astype(bf16)
    return hi, (x - hi.astype(f32)).astype(bf16)


def iota(shape, axis):
    return lax.broadcasted_iota(jnp.int32, shape, axis)


def eye():
    shape = (LANES, LANES)
    return iota(shape, 0) == iota(shape, 1)


def to_lanes(column, mask):
    return jnp.sum(jnp.where(mask, column, 0.0), axis=0, keepdims=True)


def tile(t):
    return slice(t * LANES, (t + 1) * LANES)


def features(block):
    x = block[0:FEAT]
    return jnp.where(iota(x.shape, 0) < LATENT + RANK, x, 0.0)


def half_square(block):
    x = block[0:LATENT]
    return 0.5 * jnp.sum(x * x, axis=0, keepdims=True)


def put_bias(ref, potential):
    rows = iota((16, LANES), 0)
    for t in range(potential.shape[0]):
        x = potential[t : t + 1]
        hi = x.astype(bf16).astype(f32)
        rest = x - hi
        mid = rest.astype(bf16).astype(f32)
        low = rest - mid
        block = jnp.where(rows == 0, hi, jnp.where(rows == 1, mid, jnp.where(rows == 2, low, 0.0)))
        ref[BIAS:DEPTH, tile(t)] = block.astype(bf16)


def ones_block():
    shape = (DEPTH - BIAS, LANES)
    return jnp.where(iota(shape, 0) < 3, 1.0, 0.0).astype(bf16)


def left_operand(xh, xl, moment):
    shape = (LANES, LANES)
    row, column = iota(shape, 0), iota(shape, 1)
    mixed = moment.T + jnp.where((row == column) & (row < LATENT), 1.0, 0.0)
    qh, ql = split((SCALE * mixed)[0:FEAT, 0:FEAT])
    both = dot(jnp.concatenate([qh, ql], axis=0), xh)
    return split(both[0:FEAT] + both[FEAT:] + dot(qh, xl))


def transpose_into(ref, t, block):
    unit = jnp.where(eye(), 1.0, 0.0).astype(bf16)
    ref[tile(t), :] = dot_nt(unit, block).astype(bf16)


def lse_rows(stream, fixed, out_ref, n, blocks):
    mask = eye()

    def step(b, carry):
        rows = pl.ds(pl.multiple_of(b * LANES, LANES), LANES)
        s = dot(stream[rows, :], fixed[...])
        top = s[:, tile(0)]
        for t in range(1, blocks):
            top = jnp.maximum(top, s[:, tile(t)])
        total = jnp.exp2(s[:, tile(0)] - top)
        for t in range(1, blocks):
            total = total + jnp.exp2(s[:, tile(t)] - top)
        whole = jnp.max(top, axis=1, keepdims=True)
        total = jnp.sum(total * jnp.exp2(top - whole), axis=1, keepdims=True)
        lse = to_lanes(whole + jnp.log2(total), mask)
        for k in range(n):
            out_ref[k, pl.ds(b, 1), :] = lse
        return carry

    lax.fori_loop(0, stream.shape[0] // LANES, step, 0)


def combine(parts):
    top = jnp.max(parts, axis=0)
    return top + jnp.log2(jnp.sum(jnp.exp2(parts - top[None]), axis=0))


def old_kernel(n, blocks, sg, tg, moment, lse_out, lse_own, carried, xh, xl, rt, rc, lc, b2c):
    for t in range(blocks):
        hi, low = split(features(sg[t]))
        xh[:, tile(t)] = hi
        xl[:, tile(t)] = low
        hi, low = split(features(tg[t]))
        rt[0:FEAT, tile(t)] = hi
        rt[FEAT : 2 * FEAT, tile(t)] = low
        rt[2 * FEAT : BIAS, tile(t)] = hi
        transpose_into(rc, t, jnp.concatenate([hi, low, hi, ones_block()], axis=0))
        right = jnp.concatenate([tg[t, ROW_RIGHT:PACK, :], jnp.zeros((8, LANES), f32)], axis=0)
        right = jnp.where(iota(right.shape, 0) < RANK, right, 0.0)
        hi, low = split(right)
        block = jnp.concatenate([jnp.zeros((LATENT, LANES), bf16), hi, low], axis=0)
        b2c[tile(t), :] = dot_nt(jnp.where(eye(), 1.0, 0.0).astype(bf16), block).astype(bf16)
    lh, ll = left_operand(xh[...], xl[...], moment[...])
    for t in range(blocks):
        block = jnp.concatenate([lh[:, tile(t)], lh[:, tile(t)], ll[:, tile(t)], ones_block()], axis=0)
        transpose_into(lc, t, block)
    pot = [SCALE * (tg[t, ROW_POT : ROW_POT + 1, :] - half_square(tg[t])) for t in range(blocks)]
    put_bias(rt, jnp.concatenate(pot, axis=0))
    mask = eye()

    def step(b, carry):
        rows = pl.ds(pl.multiple_of(b * LANES, LANES), LANES)
        s = dot(lc[rows, :], rt[...])
        whole = jnp.max(s, axis=1, keepdims=True)
        p = jnp.exp2(s - whole)
        total = jnp.sum(p, axis=1, keepdims=True)
        hi, low = split(p)
        c = dot(hi, b2c[...]) + dot(low, b2c[...])
        carried[rows, :] = c / total
        lse = to_lanes(whole + jnp.log2(total), mask)
        for k in range(n):
            lse_out[k, pl.ds(b, 1), :] = lse
        lse_own[pl.ds(b, 1), :] = lse
        return carry

    lax.fori_loop(0, blocks, step, 0)


def moment_kernel(n, blocks, parts, lse_own, carried, sg, f_out, moment_out):
    logw = jnp.concatenate([sg[t, ROW_LOGW : ROW_LOGW + 1, :] for t in range(blocks)], axis=0)
    f = LOG2E * logw - combine(parts[...])
    f_out[...] = f
    weight = jnp.exp2(f + lse_own[...])
    hi, low = [], []
    for t in range(blocks):
        a, b = split(sg[t, ROW_RIGHT:PACK, :] * weight[t : t + 1])
        hi.append(a)
        low.append(b)
    hi, low = jnp.concatenate(hi, axis=1), jnp.concatenate(low, axis=1)
    ch, cl = split(carried[...])
    term = dot(hi, ch) + dot(low, ch) + dot(hi, cl)
    term = term + pltpu.roll(term, LANES - 48, 1)
    for k in range(n):
        moment_out[k] = term


def sum_kernel(n, parts, out):
    total = jnp.sum(parts[...], axis=0)
    for k in range(n):
        out[k] = total


def first_g_kernel(n, blocks, parts, f, xh, xl, rc, out, lc, lt):
    total = jnp.sum(parts[...], axis=0)
    rows, lanes = iota(total.shape, 0), iota(total.shape, 1)
    keep = (rows < RANK) & (lanes >= LATENT) & (lanes < LATENT + RANK)
    total = jnp.where(keep, total, 0.0)
    moment = jnp.concatenate([jnp.zeros((LATENT, LANES), f32), total, jnp.zeros((56, LANES), f32)], axis=0)
    lh, ll = left_operand(xh[...], xl[...], moment)
    lt[0:FEAT, :] = lh
    lt[FEAT : 2 * FEAT, :] = lh
    lt[2 * FEAT : BIAS, :] = ll
    for t in range(blocks):
        transpose_into(lc, t, jnp.concatenate([lt[0:BIAS, tile(t)], ones_block()], axis=0))
    put_bias(lt, f[...])
    lse_rows(rc, lt, out, n, blocks)


def half_kernel(n, blocks, parts, gathered, stream, fixed, out, pot_out, scratch):
    logw = jnp.concatenate([gathered[t, ROW_LOGW : ROW_LOGW + 1, :] for t in range(blocks)], axis=0)
    x = LOG2E * logw - combine(parts[...])
    square = jnp.concatenate([half_square(gathered[t]) for t in range(blocks)], axis=0)
    pot_out[...] = x * (1.0 / SCALE) + square
    scratch[0:BIAS, :] = fixed[0:BIAS, :]
    put_bias(scratch, x)
    lse_rows(stream, scratch, out, n, blocks)


def last_kernel(blocks, parts, gathered, pot_out):
    logw = jnp.concatenate([gathered[t, ROW_LOGW : ROW_LOGW + 1, :] for t in range(blocks)], axis=0)
    x = LOG2E * logw - combine(parts[...])
    square = jnp.concatenate([half_square(gathered[t]) for t in range(blocks)], axis=0)
    pot_out[...] = x * (1.0 / SCALE) + square


def call(kernel, out, scratch=(), name=None):
    spec = pl.BlockSpec(memory_space=pltpu.VMEM)
    return lambda *args: pl.pallas_call(
        kernel,
        out_shape=[jax.ShapeDtypeStruct(s, d) for s, d in out],
        in_specs=[spec] * len(args),
        out_specs=[spec] * len(out),
        scratch_shapes=[pltpu.VMEM(s, d) for s, d in scratch],
        compiler_params=pltpu.CompilerParams(vmem_limit_bytes=32 * 1024 * 1024),
        name=name,
    )(*args)


def pack(latent, left, right, logw, potential):
    cells = latent.shape[0]
    rows = [latent.T, left.T, logw[None], potential[None], jnp.zeros((ROW_RIGHT - ROW_POT - 1, cells), f32)]
    return jnp.concatenate(rows + [right.T, jnp.zeros((PACK - ROW_RIGHT - RANK, cells), f32)], axis=0)


def spread(x, n):
    return jnp.broadcast_to(x[None], (n,) + x.shape)


def swap(x, axis):
    return lax.all_to_all(x, axis, 0, 0)


def shards(n_src, n_tgt, *args):
    (u, a1, b1, la, v, a2, b2, lb, g, old_moment) = args
    v, a2, b2 = (x.reshape(-1, x.shape[-1]) for x in (v, a2, b2))
    lb, g = lb.reshape(-1), g.reshape(-1)
    sg = swap(spread(pack(u, a1, b1, la, jnp.zeros_like(la)), n_tgt), "tgt")
    tg = lax.all_gather(pack(v, a2, b2, lb, g), "src", axis=0)
    bs, bt = n_tgt, n_src
    rows, cols = bs * LANES, bt * LANES
    old = jnp.pad(old_moment, ((LATENT, LANES - LATENT - RANK),) * 2)

    lse, own, carried, xh, xl, rt, rc = call(
        functools.partial(old_kernel, n_tgt, bs),
        [
            ((n_tgt, bs, LANES), f32),
            ((bs, LANES), f32),
            ((rows, LANES), f32),
            ((FEAT, rows), bf16),
            ((FEAT, rows), bf16),
            ((DEPTH, cols), bf16),
            ((cols, DEPTH), bf16),
        ],
        [((rows, DEPTH), bf16), ((cols, LANES), bf16)],
        name="old_plan",
    )(sg, tg, old)
    f, moment = call(
        functools.partial(moment_kernel, n_tgt, bs),
        [((bs, LANES), f32), ((n_tgt, PACK - ROW_RIGHT, LANES), f32)],
        name="moment",
    )(swap(lse, "tgt"), own, carried, sg)
    (moment,) = call(
        functools.partial(sum_kernel, n_src),
        [((n_src, PACK - ROW_RIGHT, LANES), f32)],
        name="moment_sum",
    )(swap(moment, "tgt"))
    part, lc, lt = call(
        functools.partial(first_g_kernel, n_src, bs),
        [((n_src, bt, LANES), f32), ((rows, DEPTH), bf16), ((DEPTH, rows), bf16)],
        name="first_g",
    )(swap(moment, "src"), f, xh, xl, rc)
    half = lambda n, b, cells, name: call(
        functools.partial(half_kernel, n, b),
        [((n, b, LANES), f32), ((b, LANES), f32)],
        [((DEPTH, cells), bf16)],
        name=name,
    )
    part, _ = half(n_tgt, bt, cols, "first_f")(swap(part, "src"), tg, lc, rt)
    part, _ = half(n_src, bs, rows, "second_g")(swap(part, "tgt"), sg, rc, lt)
    part, g = half(n_tgt, bt, cols, "second_f")(swap(part, "src"), tg, lc, rt)
    (f,) = call(functools.partial(last_kernel, bs), [((bs, LANES), f32)], name="last_f")(swap(part, "tgt"), sg)
    return f.reshape(-1), g.reshape(-1)


def solution(mesh):
    return jax.shard_map(
        functools.partial(shards, mesh.shape["src"], mesh.shape["tgt"]),
        mesh=mesh,
        in_specs=(
            P(("src", "tgt"), None),
            P(("src", "tgt"), None),
            P(("src", "tgt"), None),
            P(("src", "tgt")),
            P("tgt", "src", None, None),
            P("tgt", "src", None, None),
            P("tgt", "src", None, None),
            P("tgt", "src", None),
            P("tgt", "src", None),
            P(),
        ),
        out_specs=(P("src"), P("tgt")),
        check_vma=False,
    )
```

```python
import functools

import jax
import jax.numpy as jnp
from jax import lax
from jax.experimental import pallas as pl
from jax.experimental.pallas import tpu as pltpu
from jax.sharding import PartitionSpec as P

LATENT = 32
RANK = 34
FEAT = 80
BIAS = 3 * FEAT
DEPTH = 256
LANES = 128
ENTROPY = 0.1
LOG2E = 1.4426950408889634
SCALE = LOG2E / ENTROPY

ROW_LOGW = LATENT + RANK
ROW_POT = ROW_LOGW + 1
ROW_RIGHT = 72
PACK = 112
RIGHT = 48
MOMENT = 40
CHUNK = 256

f32 = jnp.float32
bf16 = jnp.bfloat16


def dot(a, b):
    return jnp.dot(a, b, preferred_element_type=f32)


def dot_nt(a, b):
    return lax.dot_general(a, b, (((1,), (1,)), ((), ())), preferred_element_type=f32)


def split(x):
    hi = x.astype(bf16)
    return hi, (x - hi.astype(f32)).astype(bf16)


def iota(shape, axis):
    return lax.broadcasted_iota(jnp.int32, shape, axis)


def eye():
    shape = (LANES, LANES)
    return iota(shape, 0) == iota(shape, 1)


def to_lanes(column, mask):
    return jnp.sum(jnp.where(mask, column, 0.0), axis=0, keepdims=True)


def tile(t):
    return slice(t * LANES, (t + 1) * LANES)


def features(block):
    x = block[0:FEAT]
    return jnp.where(iota(x.shape, 0) < LATENT + RANK, x, 0.0)


def pick(x, row, n):
    return jnp.concatenate([x[t, row : row + 1, :] for t in range(n)], axis=0)


def half_square(block):
    x = block[0:LATENT]
    return 0.5 * jnp.sum(x * x, axis=0, keepdims=True)


def three(x):
    hi = x.astype(bf16).astype(f32)
    rest = x - hi
    mid = rest.astype(bf16).astype(f32)
    return hi, mid, rest - mid


def extra(terms):
    rows = iota((DEPTH - BIAS, LANES), 0)
    out = jnp.zeros(rows.shape, f32)
    for k, x in terms.items():
        out = jnp.where(rows == k, x, out)
    return out.astype(bf16)


ONES = {0: 1.0, 1: 1.0, 2: 1.0}


def put_bias(ref, potential):
    for t in range(potential.shape[0]):
        ref[BIAS:DEPTH, tile(t)] = extra(dict(enumerate(three(potential[t : t + 1]))))


def left_operand(xh, xl, moment):
    shape = (LANES, LANES)
    row, column = iota(shape, 0), iota(shape, 1)
    mixed = moment.T + jnp.where((row == column) & (row < LATENT), 1.0, 0.0)
    qh, ql = split((SCALE * mixed)[0:FEAT, 0:FEAT])
    both = dot(jnp.concatenate([qh, ql], axis=0), xh)
    return split(both[0:FEAT] + both[FEAT:] + dot(qh, xl))


def transpose_into(ref, t, block):
    unit = jnp.where(eye(), 1.0, 0.0).astype(bf16)
    ref[tile(t), :] = dot_nt(unit, block).astype(bf16)


def reduce_rows(s, row, mask):
    tops, totals = [], []
    for k in range(0, LANES, 8):
        x = [s[row + k : row + k + 8, tile(t)] for t in range(s.shape[1] // LANES)]
        top = functools.reduce(jnp.maximum, x)
        tops.append(top)
        totals.append(functools.reduce(jnp.add, [jnp.exp2(y - top) for y in x]))
    top, total = jnp.concatenate(tops, axis=0), jnp.concatenate(totals, axis=0)
    whole = jnp.max(top, axis=1, keepdims=True)
    total = jnp.sum(total * jnp.exp2(top - whole), axis=1, keepdims=True)
    return to_lanes(whole + jnp.log2(total), mask)


def lse_rows(stream, fixed, out_ref, n, s0, s1, held):
    mask = eye()
    s = (s0, s1)
    steps = stream.shape[0] // CHUNK
    s0[...] = dot(stream[0:CHUNK, :], fixed[...])
    for b in range(steps):
        if b + 1 < steps:
            s[(b + 1) % 2][...] = dot(stream[(b + 1) * CHUNK : (b + 2) * CHUNK, :], fixed[...])
        for k in range(CHUNK // LANES):
            t = b * (CHUNK // LANES) + k
            held[t : t + 1, :] = reduce_rows(s[b % 2], k * LANES, mask)
    for k in range(n):
        out_ref[k] = held[...]


def combine(parts):
    top = jnp.max(parts, axis=0)
    return top + jnp.log2(jnp.sum(jnp.exp2(parts - top[None]), axis=0))


def pack_kernel(n, u, a1, b1, la, v, a2, b2, lb, g, source, target):
    def rows(latent, left, right, logw, pot):
        return [
            (0, latent[...]),
            (LATENT, left[...]),
            (ROW_LOGW, logw[...]),
            (ROW_POT, pot),
            (ROW_POT + 1, jnp.zeros((ROW_RIGHT - ROW_POT - 1, LANES), f32)),
            (ROW_RIGHT, right[...]),
            (ROW_RIGHT + RANK, jnp.zeros((PACK - ROW_RIGHT - RANK, LANES), f32)),
        ]

    for at, x in rows(v, a2, b2, lb, g[...]):
        target[at : at + x.shape[0], :] = x
    for at, x in rows(u, a1, b1, la, jnp.zeros((1, LANES), f32)):
        for k in range(n):
            source[k, at : at + x.shape[0], :] = x


def old_kernel(n, blocks, sg, tg, moment, lse_out, lse_own, carried, xh, xl, rt, rc, lt, b2, s0, s1, ph, pl_, held):
    for t in range(blocks):
        hi, low = split(features(tg[t]))
        rt[0:FEAT, tile(t)] = hi
        rt[FEAT : 2 * FEAT, tile(t)] = low
        rt[2 * FEAT : BIAS, tile(t)] = hi
        pot = SCALE * (tg[t, ROW_POT : ROW_POT + 1, :] - half_square(tg[t]))
        more = extra(ONES | {3 + k: x for k, x in enumerate(three(pot))})
        transpose_into(rc, t, jnp.concatenate([hi, low, hi, more], axis=0))
        right = jnp.concatenate([tg[t, ROW_RIGHT:PACK, :], jnp.zeros((RIGHT + ROW_RIGHT - PACK, LANES), f32)], axis=0)
        hi, low = split(right)
        b2[0:RIGHT, tile(t)] = hi
        b2[RIGHT:, tile(t)] = low
        hi, low = split(features(sg[t]))
        xh[:, tile(t)] = hi
        xl[:, tile(t)] = low
        lt[BIAS:DEPTH, tile(t)] = extra({3: 1.0, 4: 1.0, 5: 1.0})
    lh, ll = left_operand(xh[...], xl[...], moment[...])
    lt[0:FEAT, :] = lh
    lt[FEAT : 2 * FEAT, :] = lh
    lt[2 * FEAT : BIAS, :] = ll
    cells, piece = rc.shape[0], 64
    steps = lt.shape[1] // CHUNK

    def columns(b):
        return pl.ds(pl.multiple_of(b * CHUNK, CHUNK), CHUNK)

    def scores(b, s):
        s[...] = dot(rc[...], lt[:, columns(b)])

    def plan(b, s):
        top = s[0:piece, :]
        for k in range(piece, cells, piece):
            top = jnp.maximum(top, s[k : k + piece, :])
        top = jnp.max(top, axis=0, keepdims=True)
        total = jnp.zeros((piece, CHUNK), f32)
        for k in range(0, cells, piece):
            p = jnp.exp2(s[k : k + piece, :] - top)
            total = total + p
            hi, low = split(p)
            ph[k : k + piece, :] = hi
            pl_[k : k + piece, :] = low
        total = jnp.sum(total, axis=0, keepdims=True)
        c = dot(b2[...], ph[...])
        c = c[0:RIGHT] + c[RIGHT:] + dot(b2[0:RIGHT, :], pl_[...])
        carried[:, columns(b)] = c / total
        held[:, columns(b)] = top + jnp.log2(total)

    scores(0, s0)

    def step(i, carry):
        scores(2 * i + 1, s1)
        plan(2 * i, s0)
        scores(lax.rem(2 * i + 2, steps), s0)
        plan(2 * i + 1, s1)
        return carry

    lax.fori_loop(0, steps // 2, step, 0)
    lse = jnp.concatenate([held[:, tile(t)] for t in range(cells // LANES)], axis=0)
    lse_own[...] = lse
    for k in range(n):
        lse_out[k] = lse


def moment_kernel(n, blocks, parts, lse_own, carried, sg, f_out, moment_out):
    f = LOG2E * pick(sg, ROW_LOGW, blocks) - combine(parts[...])
    f_out[...] = f
    weight = jnp.exp2(f + lse_own[...])
    left = [sg[t, ROW_RIGHT:PACK, :] * weight[t : t + 1] for t in range(blocks)]
    hi, low = split(jnp.concatenate(left, axis=1))
    ch, cl = split(carried[...])
    fill = jnp.zeros((LANES - RIGHT, ch.shape[1]), bf16)
    ch, cl = jnp.concatenate([ch, fill], axis=0), jnp.concatenate([cl, fill], axis=0)
    x = dot_nt(hi, ch) + dot_nt(low, ch) + dot_nt(hi, cl)
    second, third = pltpu.roll(x[16:32], MOMENT, 1), pltpu.roll(x[32:40], 2 * MOMENT, 1)
    packed = x[0:16] + second + jnp.concatenate([third, jnp.zeros_like(third)], axis=0)
    for k in range(n):
        moment_out[k] = packed


def sum_kernel(n, parts, out):
    total = jnp.sum(parts[...], axis=0)
    for k in range(n):
        out[k] = total


def unpack_moment(packed):
    first = pltpu.roll(packed, LATENT, 1)
    second = pltpu.roll(packed, LANES + LATENT - MOMENT, 1)
    third = pltpu.roll(packed[0:8], LANES + LATENT - 2 * MOMENT, 1)
    x = jnp.concatenate([first, second, third], axis=0)
    rows, lanes = iota(x.shape, 0), iota(x.shape, 1)
    x = jnp.where((rows < RANK) & (lanes >= LATENT) & (lanes < LATENT + RANK), x, 0.0)
    return jnp.concatenate([jnp.zeros((LATENT, LANES), f32), x, jnp.zeros((LANES - LATENT - MOMENT, LANES), f32)], axis=0)


def first_g_kernel(n, blocks, parts, f, xh, xl, rc, out, lc, lt, s0, s1, held):
    moment = unpack_moment(jnp.sum(parts[...], axis=0))
    lh, ll = left_operand(xh[...], xl[...], moment)
    lt[0:FEAT, :] = lh
    lt[FEAT : 2 * FEAT, :] = lh
    lt[2 * FEAT : BIAS, :] = ll
    put_bias(lt, f[...])
    for t in range(blocks):
        transpose_into(lc, t, jnp.concatenate([lt[0:BIAS, tile(t)], extra(ONES)], axis=0))
    lse_rows(rc, lt, out, n, s0, s1, held)


def potential(blocks, parts, gathered):
    x = LOG2E * pick(gathered, ROW_LOGW, blocks) - combine(parts[...])
    square = jnp.concatenate([half_square(gathered[t]) for t in range(blocks)], axis=0)
    return x, x * (1.0 / SCALE) + square


def half_kernel(n, blocks, parts, gathered, stream, fixed_in, out, pot_out, fixed, s0, s1, held):
    x, pot_out[...] = potential(blocks, parts, gathered)
    put_bias(fixed, x)
    lse_rows(stream, fixed, out, n, s0, s1, held)


def last_kernel(blocks, parts, gathered, pot_out):
    _, pot_out[...] = potential(blocks, parts, gathered)


def call(kernel, out, scratch=(), name=None, aliases={}):
    spec = pl.BlockSpec(memory_space=pltpu.VMEM)
    return lambda *args: pl.pallas_call(
        kernel,
        out_shape=[jax.ShapeDtypeStruct(s, d) for s, d in out],
        in_specs=[spec] * len(args),
        out_specs=[spec] * len(out),
        scratch_shapes=[pltpu.VMEM(s, d) for s, d in scratch],
        input_output_aliases=aliases,
        compiler_params=pltpu.CompilerParams(vmem_limit_bytes=32 * 1024 * 1024),
        name=name,
    )(*args)


def swap(x, axis):
    return lax.all_to_all(x, axis, 0, 0)


def shards(n_src, n_tgt, *args):
    (u, a1, b1, la, v, a2, b2, lb, g, old_moment) = args
    v, a2, b2 = (x.reshape(-1, x.shape[-1]) for x in (v, a2, b2))
    flat = lambda x: x.reshape(1, -1)
    source, target = call(
        functools.partial(pack_kernel, n_tgt),
        [((n_tgt, PACK, LANES), f32), ((PACK, LANES), f32)],
        name="pack",
    )(u.T, a1.T, b1.T, flat(la), v.T, a2.T, b2.T, flat(lb), flat(g))
    sg = swap(source, "tgt")
    tg = lax.all_gather(target, "src", axis=0)
    bs, bt = n_tgt, n_src
    rows, cols = bs * LANES, bt * LANES
    old = jnp.pad(old_moment, ((LATENT, LANES - LATENT - RANK),) * 2)

    lse, own, carried, xh, xl, rt, rc = call(
        functools.partial(old_kernel, n_tgt, bs),
        [
            ((n_tgt, bs, LANES), f32),
            ((bs, LANES), f32),
            ((RIGHT, rows), f32),
            ((FEAT, rows), bf16),
            ((FEAT, rows), bf16),
            ((DEPTH, cols), bf16),
            ((cols, DEPTH), bf16),
        ],
        [
            ((DEPTH, rows), bf16),
            ((2 * RIGHT, cols), bf16),
            ((cols, CHUNK), f32),
            ((cols, CHUNK), f32),
            ((cols, CHUNK), bf16),
            ((cols, CHUNK), bf16),
            ((1, rows), f32),
        ],
        name="old_plan",
    )(sg, tg, old)
    f, moment = call(
        functools.partial(moment_kernel, n_tgt, bs),
        [((bs, LANES), f32), ((n_tgt, 16, LANES), f32)],
        name="moment",
    )(swap(lse, "tgt"), own, carried, sg)
    (moment,) = call(functools.partial(sum_kernel, n_src), [((n_src, 16, LANES), f32)], name="moment_sum")(
        swap(moment, "tgt")
    )
    pipe = lambda cells, b: [((CHUNK, cells), f32), ((CHUNK, cells), f32), ((b, LANES), f32)]
    part, lc, lt = call(
        functools.partial(first_g_kernel, n_src, bs),
        [((n_src, bt, LANES), f32), ((rows, DEPTH), bf16), ((DEPTH, rows), bf16)],
        pipe(rows, bt),
        name="first_g",
    )(swap(moment, "src"), f, xh, xl, rc)
    half = lambda n, fixed, streamed, name: call(
        functools.partial(half_kernel, n, fixed),
        [((n, streamed, LANES), f32), ((fixed, LANES), f32), ((DEPTH, fixed * LANES), bf16)],
        pipe(fixed * LANES, streamed),
        name=name,
        aliases={3: 2},
    )
    part, _, rt = half(n_tgt, bt, bs, "first_f")(swap(part, "src"), tg, lc, rt)
    part, _, lt = half(n_src, bs, bt, "second_g")(swap(part, "tgt"), sg, rc, lt)
    part, g, rt = half(n_tgt, bt, bs, "second_f")(swap(part, "src"), tg, lc, rt)
    (f,) = call(functools.partial(last_kernel, bs), [((bs, LANES), f32)], name="last_f")(swap(part, "tgt"), sg)
    return f.reshape(-1), g.reshape(-1)


def solution(mesh):
    return jax.shard_map(
        functools.partial(shards, mesh.shape["src"], mesh.shape["tgt"]),
        mesh=mesh,
        in_specs=(
            P(("src", "tgt"), None),
            P(("src", "tgt"), None),
            P(("src", "tgt"), None),
            P(("src", "tgt")),
            P("tgt", "src", None, None),
            P("tgt", "src", None, None),
            P("tgt", "src", None, None),
            P("tgt", "src", None),
            P("tgt", "src", None),
            P(),
        ),
        out_specs=(P("src"), P("tgt")),
        check_vma=False,
    )
```

```python
import functools

import jax
import jax.numpy as jnp
from jax import lax
from jax.experimental import pallas as pl
from jax.experimental.pallas import tpu as pltpu
from jax.sharding import PartitionSpec as P

LATENT = 32
RANK = 34
FEAT = 80
BIAS = 3 * FEAT
DEPTH = 256
LANES = 128
ENTROPY = 0.1
LOG2E = 1.4426950408889634
SCALE = LOG2E / ENTROPY

ROW_LOGW = LATENT + RANK
ROW_POT = ROW_LOGW + 1
ROW_RIGHT = 72
PACK = 112
RIGHT = 48
MOMENT = 40
CHUNK = 256
HEADROOM = 100.0
SMALLEST = 2.0**-99
LARGEST = 2.0**126

f32 = jnp.float32
bf16 = jnp.bfloat16


def dot(a, b):
    return jnp.dot(a, b, preferred_element_type=f32)


def dot_nt(a, b):
    return lax.dot_general(a, b, (((1,), (1,)), ((), ())), preferred_element_type=f32)


def split(x):
    hi = x.astype(bf16)
    return hi, (x - hi.astype(f32)).astype(bf16)


def iota(shape, axis):
    return lax.broadcasted_iota(jnp.int32, shape, axis)


def eye():
    shape = (LANES, LANES)
    return iota(shape, 0) == iota(shape, 1)


def to_lanes(column, mask):
    return jnp.sum(jnp.where(mask, column, 0.0), axis=0, keepdims=True)


def tile(t):
    return slice(t * LANES, (t + 1) * LANES)


def features(block):
    x = block[0:FEAT]
    return jnp.where(iota(x.shape, 0) < LATENT + RANK, x, 0.0)


def pick(x, row, n):
    return jnp.concatenate([x[t, row : row + 1, :] for t in range(n)], axis=0)


def half_square(block):
    x = block[0:LATENT]
    return 0.5 * jnp.sum(x * x, axis=0, keepdims=True)


def three(x):
    hi = x.astype(bf16).astype(f32)
    rest = x - hi
    mid = rest.astype(bf16).astype(f32)
    return hi, mid, rest - mid


def extra(terms):
    rows = iota((DEPTH - BIAS, LANES), 0)
    out = jnp.zeros(rows.shape, f32)
    for k, x in terms.items():
        out = jnp.where(rows == k, x, out)
    return out.astype(bf16)


ONES = {0: 1.0, 1: 1.0, 2: 1.0}


def put_bias(ref, potential, more={}):
    for t in range(potential.shape[0]):
        ref[BIAS:DEPTH, tile(t)] = extra(dict(enumerate(three(potential[t : t + 1]))) | more)


def shifted(shift):
    return extra(ONES | {3 + k: x for k, x in enumerate(three(shift))})


def left_operand(xh, xl, moment):
    shape = (LANES, LANES)
    row, column = iota(shape, 0), iota(shape, 1)
    mixed = moment.T + jnp.where((row == column) & (row < LATENT), 1.0, 0.0)
    qh, ql = split((SCALE * mixed)[0:FEAT, 0:FEAT])
    both = dot(jnp.concatenate([qh, ql], axis=0), xh)
    return split(both[0:FEAT] + both[FEAT:] + dot(qh, xl))


def transpose_into(ref, t, block):
    unit = jnp.where(eye(), 1.0, 0.0).astype(bf16)
    ref[tile(t), :] = dot_nt(unit, block).astype(bf16)


def restream(ref, t, fixed, shift):
    unit = jnp.where(eye(), 1.0, 0.0).astype(bf16)
    block = jnp.concatenate([fixed[LANES:BIAS, tile(t)], shifted(shift)], axis=0)
    ref[tile(t), LANES:DEPTH] = dot_nt(unit, block).astype(bf16)


def reduce_rows(s, row, mask):
    tops, totals = [], []
    for k in range(0, LANES, 8):
        x = [s[row + k : row + k + 8, tile(t)] for t in range(s.shape[1] // LANES)]
        top = functools.reduce(jnp.maximum, x)
        tops.append(top)
        totals.append(functools.reduce(jnp.add, [jnp.exp2(y - top) for y in x]))
    top, total = jnp.concatenate(tops, axis=0), jnp.concatenate(totals, axis=0)
    whole = jnp.max(top, axis=1, keepdims=True)
    total = jnp.sum(total * jnp.exp2(top - whole), axis=1, keepdims=True)
    return to_lanes(whole, mask), to_lanes(total, mask)


def add_rows(s, row, mask):
    totals = []
    for k in range(0, LANES, 8):
        x = [jnp.exp2(s[row + k : row + k + 8, tile(t)]) for t in range(s.shape[1] // LANES)]
        totals.append(functools.reduce(jnp.add, x))
    return to_lanes(jnp.sum(jnp.concatenate(totals, axis=0), axis=1, keepdims=True), mask)


def pipeline(stream, fixed, s0, s1, reduce):
    s = (s0, s1)
    steps = stream.shape[0] // CHUNK
    s0[...] = dot(stream[0:CHUNK, :], fixed[...])
    for b in range(steps):
        if b + 1 < steps:
            s[(b + 1) % 2][...] = dot(stream[(b + 1) * CHUNK : (b + 2) * CHUNK, :], fixed[...])
        for k in range(CHUNK // LANES):
            reduce(b * (CHUNK // LANES) + k, s[b % 2], k * LANES)


def lse_rows(stream, fixed, out_ref, n, s0, s1, tops, totals):
    mask = eye()

    def reduce(t, s, row):
        tops[t : t + 1, :], totals[t : t + 1, :] = reduce_rows(s, row, mask)

    pipeline(stream, fixed, s0, s1, reduce)
    lse = tops[...] + jnp.log2(totals[...])
    for k in range(n):
        out_ref[k] = lse


def shifted_lse_rows(stream, fixed, shift, out_ref, n, s0, s1, tops, totals):
    mask = eye()

    def reduce(t, s, row):
        totals[t : t + 1, :] = add_rows(s, row, mask)

    pipeline(stream, fixed, s0, s1, reduce)
    total = totals[...]
    tops[...] = jnp.log2(total)
    good = jnp.all((total >= SMALLEST) & (total <= LARGEST))

    @pl.when(jnp.logical_not(good))
    def _():
        def step(t, carry):
            s0[0:LANES, :] = dot(stream[pl.ds(pl.multiple_of(t * LANES, LANES), LANES), :], fixed[...])
            top, total = reduce_rows(s0, 0, mask)
            tops[pl.ds(t, 1), :] = top + jnp.log2(total)
            return carry

        lax.fori_loop(0, stream.shape[0] // LANES, step, 0)

    lse = tops[...] - shift
    for k in range(n):
        out_ref[k] = lse


def combine(parts):
    top = jnp.max(parts, axis=0)
    return top + jnp.log2(jnp.sum(jnp.exp2(parts - top[None]), axis=0))


def pack_kernel(n, u, a1, b1, la, v, a2, b2, lb, g, source, target):
    def rows(latent, left, right, logw, pot):
        zero = jnp.zeros((ROW_RIGHT - ROW_POT - 1, LANES), f32)
        fill = jnp.zeros((PACK - ROW_RIGHT - RANK, LANES), f32)
        return jnp.concatenate([latent, left, logw, pot, zero, right, fill], axis=0)

    target[...] = rows(v[...], a2[:, 0, :], b2[:, 0, :], lb[...], g[...])
    x = rows(u[...], a1[...], b1[...], la[...], jnp.zeros((1, LANES), f32))
    for k in range(n):
        source[k] = x


def old_kernel(n, blocks, sg, tg, moment, lse_out, lse_own, carried, xh, xl, rt, rc, lt, b2, s0, s1, ph, pl_, held):
    for t in range(blocks):
        hi, low = split(features(tg[t]))
        rt[0:FEAT, tile(t)] = hi
        rt[FEAT : 2 * FEAT, tile(t)] = low
        rt[2 * FEAT : BIAS, tile(t)] = hi
        pot = SCALE * (tg[t, ROW_POT : ROW_POT + 1, :] - half_square(tg[t]))
        transpose_into(rc, t, jnp.concatenate([hi, low, hi, shifted(pot)], axis=0))
        right = jnp.concatenate([tg[t, ROW_RIGHT:PACK, :], jnp.zeros((RIGHT + ROW_RIGHT - PACK, LANES), f32)], axis=0)
        hi, low = split(right)
        b2[0:RIGHT, tile(t)] = hi
        b2[RIGHT:, tile(t)] = low
        hi, low = split(features(sg[t]))
        xh[:, tile(t)] = hi
        xl[:, tile(t)] = low
        lt[BIAS:DEPTH, tile(t)] = extra({3: 1.0, 4: 1.0, 5: 1.0})
    lh, ll = left_operand(xh[...], xl[...], moment[...])
    lt[0:FEAT, :] = lh
    lt[FEAT : 2 * FEAT, :] = lh
    lt[2 * FEAT : BIAS, :] = ll
    cells, piece = rc.shape[0], 64
    steps = lt.shape[1] // CHUNK

    def columns(b):
        return pl.ds(pl.multiple_of(b * CHUNK, CHUNK), CHUNK)

    def scores(b, s):
        s[...] = dot(rc[...], lt[:, columns(b)])

    def plan(b, s):
        top = s[0:piece, :]
        for k in range(piece, cells, piece):
            top = jnp.maximum(top, s[k : k + piece, :])
        top = jnp.max(top, axis=0, keepdims=True)
        total = jnp.zeros((piece, CHUNK), f32)
        for k in range(0, cells, piece):
            p = jnp.exp2(s[k : k + piece, :] - top)
            total = total + p
            hi, low = split(p)
            ph[k : k + piece, :] = hi
            pl_[k : k + piece, :] = low
        total = jnp.sum(total, axis=0, keepdims=True)
        c = dot(b2[...], ph[...])
        c = c[0:RIGHT] + c[RIGHT:] + dot(b2[0:RIGHT, :], pl_[...])
        carried[:, columns(b)] = c / total
        held[:, columns(b)] = top + jnp.log2(total)

    scores(0, s0)

    def step(i, carry):
        scores(2 * i + 1, s1)
        plan(2 * i, s0)
        scores(lax.rem(2 * i + 2, steps), s0)
        plan(2 * i + 1, s1)
        return carry

    lax.fori_loop(0, steps // 2, step, 0)
    lse = jnp.concatenate([held[:, tile(t)] for t in range(cells // LANES)], axis=0)
    lse_own[...] = lse
    for k in range(n):
        lse_out[k] = lse


def moment_kernel(n, blocks, parts, lse_own, carried, sg, f_out, moment_out):
    f = LOG2E * pick(sg, ROW_LOGW, blocks) - combine(parts[...])
    f_out[...] = f
    weight = jnp.exp2(f + lse_own[...])
    left = [sg[t, ROW_RIGHT:PACK, :] * weight[t : t + 1] for t in range(blocks)]
    hi, low = split(jnp.concatenate(left, axis=1))
    ch, cl = split(carried[...])
    fill = jnp.zeros((LANES - RIGHT, ch.shape[1]), bf16)
    ch, cl = jnp.concatenate([ch, fill], axis=0), jnp.concatenate([cl, fill], axis=0)
    x = dot_nt(hi, ch) + dot_nt(low, ch) + dot_nt(hi, cl)
    second, third = pltpu.roll(x[16:32], MOMENT, 1), pltpu.roll(x[32:40], 2 * MOMENT, 1)
    packed = x[0:16] + second + jnp.concatenate([third, jnp.zeros_like(third)], axis=0)
    for k in range(n):
        moment_out[k] = packed


def sum_kernel(n, parts, out):
    total = jnp.sum(parts[...], axis=0)
    for k in range(n):
        out[k] = total


def unpack_moment(packed):
    first = pltpu.roll(packed, LATENT, 1)
    second = pltpu.roll(packed, LANES + LATENT - MOMENT, 1)
    third = pltpu.roll(packed[0:8], LANES + LATENT - 2 * MOMENT, 1)
    x = jnp.concatenate([first, second, third], axis=0)
    rows, lanes = iota(x.shape, 0), iota(x.shape, 1)
    x = jnp.where((rows < RANK) & (lanes >= LATENT) & (lanes < LATENT + RANK), x, 0.0)
    return jnp.concatenate([jnp.zeros((LATENT, LANES), f32), x, jnp.zeros((LANES - LATENT - MOMENT, LANES), f32)], axis=0)


def first_g_kernel(n, blocks, parts, f, xh, xl, rc, out, lc, lt, s0, s1, tops, totals):
    moment = unpack_moment(jnp.sum(parts[...], axis=0))
    lh, ll = left_operand(xh[...], xl[...], moment)
    lt[0:FEAT, :] = lh
    lt[FEAT : 2 * FEAT, :] = lh
    lt[2 * FEAT : BIAS, :] = ll
    put_bias(lt, f[...])
    for t in range(blocks):
        more = shifted(f[t : t + 1, :] + HEADROOM)
        transpose_into(lc, t, jnp.concatenate([lt[0:BIAS, tile(t)], more], axis=0))
    lse_rows(rc, lt, out, n, s0, s1, tops, totals)


def updated(blocks, parts, gathered):
    return LOG2E * pick(gathered, ROW_LOGW, blocks) - combine(parts[...])


def potential(blocks, x, gathered):
    return x * (1.0 / SCALE) + jnp.concatenate([half_square(gathered[t]) for t in range(blocks)], axis=0)


def half_kernel(n, blocks, parts, gathered, old, stream, fixed_in, other_in, out, x_out, fixed, other, *scratch):
    x = updated(blocks, parts, gathered)
    x_out[...] = x
    put_bias(fixed, x, {3: 1.0, 4: 1.0, 5: 1.0})
    for t in range(blocks):
        restream(other, t, fixed, x[t : t + 1] + HEADROOM)
    shifted_lse_rows(stream, fixed, old[...] + HEADROOM, out, n, *scratch)


def last_half_kernel(n, blocks, parts, gathered, old, stream, fixed_in, out, pot_out, fixed, *scratch):
    x = updated(blocks, parts, gathered)
    pot_out[...] = potential(blocks, x, gathered)
    put_bias(fixed, x, {3: 1.0, 4: 1.0, 5: 1.0})
    shifted_lse_rows(stream, fixed, old[...] + HEADROOM, out, n, *scratch)


def last_kernel(blocks, parts, gathered, pot_out):
    pot_out[...] = potential(blocks, updated(blocks, parts, gathered), gathered)


def call(kernel, out, scratch=(), name=None, aliases={}):
    spec = pl.BlockSpec(memory_space=pltpu.VMEM)
    return lambda *args: pl.pallas_call(
        kernel,
        out_shape=[jax.ShapeDtypeStruct(s, d) for s, d in out],
        in_specs=[spec] * len(args),
        out_specs=[spec] * len(out),
        scratch_shapes=[pltpu.VMEM(s, d) for s, d in scratch],
        input_output_aliases=aliases,
        compiler_params=pltpu.CompilerParams(vmem_limit_bytes=32 * 1024 * 1024),
        name=name,
    )(*args)


def swap(x, axis):
    return lax.all_to_all(x, axis, 0, 0)


def shards(n_src, n_tgt, *args):
    (u, a1, b1, la, v, a2, b2, lb, g, old_moment) = args
    v = v.reshape(v.shape[2:])
    a2, b2 = (x.transpose(3, 0, 1, 2).reshape(x.shape[3], 1, -1) for x in (a2, b2))
    flat = lambda x: x.reshape(1, -1)
    source, target = call(
        functools.partial(pack_kernel, n_tgt),
        [((n_tgt, PACK, LANES), f32), ((PACK, LANES), f32)],
        name="pack",
    )(u.T, a1.T, b1.T, flat(la), v.T, a2, b2, flat(lb), flat(g))
    sg = swap(source, "tgt")
    tg = lax.all_gather(target, "src", axis=0)
    bs, bt = n_tgt, n_src
    rows, cols = bs * LANES, bt * LANES
    old = jnp.pad(old_moment, ((LATENT, LANES - LATENT - RANK),) * 2)

    lse, own, carried, xh, xl, rt, rc = call(
        functools.partial(old_kernel, n_tgt, bs),
        [
            ((n_tgt, bs, LANES), f32),
            ((bs, LANES), f32),
            ((RIGHT, rows), f32),
            ((FEAT, rows), bf16),
            ((FEAT, rows), bf16),
            ((DEPTH, cols), bf16),
            ((cols, DEPTH), bf16),
        ],
        [
            ((DEPTH, rows), bf16),
            ((2 * RIGHT, cols), bf16),
            ((cols, CHUNK), f32),
            ((cols, CHUNK), f32),
            ((cols, CHUNK), bf16),
            ((cols, CHUNK), bf16),
            ((1, rows), f32),
        ],
        name="old_plan",
    )(sg, tg, old)
    f, moment = call(
        functools.partial(moment_kernel, n_tgt, bs),
        [((bs, LANES), f32), ((n_tgt, 16, LANES), f32)],
        name="moment",
    )(swap(lse, "tgt"), own, carried, sg)
    (moment,) = call(functools.partial(sum_kernel, n_src), [((n_src, 16, LANES), f32)], name="moment_sum")(
        swap(moment, "tgt")
    )
    pipe = lambda cells, b: [((CHUNK, cells), f32)] * 2 + [((b, LANES), f32)] * 2
    part, lc, lt = call(
        functools.partial(first_g_kernel, n_src, bs),
        [((n_src, bt, LANES), f32), ((rows, DEPTH), bf16), ((DEPTH, rows), bf16)],
        pipe(rows, bt),
        name="first_g",
    )(swap(moment, "src"), f, xh, xl, rc)
    half = lambda n, fixed, streamed, name: call(
        functools.partial(half_kernel, n, fixed),
        [
            ((n, streamed, LANES), f32),
            ((fixed, LANES), f32),
            ((DEPTH, fixed * LANES), bf16),
            ((fixed * LANES, DEPTH), bf16),
        ],
        pipe(fixed * LANES, streamed),
        name=name,
        aliases={4: 2, 5: 3},
    )
    part, g, rt, rc = half(n_tgt, bt, bs, "first_f")(swap(part, "src"), tg, f, lc, rt, rc)
    part, f, lt, lc = half(n_src, bs, bt, "second_g")(swap(part, "tgt"), sg, g, rc, lt, lc)
    part, g, _ = call(
        functools.partial(last_half_kernel, n_tgt, bt),
        [((n_tgt, bs, LANES), f32), ((bt, LANES), f32), ((DEPTH, cols), bf16)],
        pipe(cols, bs),
        name="second_f",
        aliases={4: 2},
    )(swap(part, "src"), tg, f, lc, rt)
    (f,) = call(functools.partial(last_kernel, bs), [((bs, LANES), f32)], name="last_f")(swap(part, "tgt"), sg)
    return f.reshape(-1), g.reshape(-1)


def solution(mesh):
    return jax.shard_map(
        functools.partial(shards, mesh.shape["src"], mesh.shape["tgt"]),
        mesh=mesh,
        in_specs=(
            P(("src", "tgt"), None),
            P(("src", "tgt"), None),
            P(("src", "tgt"), None),
            P(("src", "tgt")),
            P("tgt", "src", None, None),
            P("tgt", "src", None, None),
            P("tgt", "src", None, None),
            P("tgt", "src", None),
            P("tgt", "src", None),
            P(),
        ),
        out_specs=(P("src"), P("tgt")),
        check_vma=False,
    )
```

```python
import functools

import jax
import jax.numpy as jnp
from jax import lax
from jax.experimental import pallas as pl
from jax.experimental.pallas import tpu as pltpu
from jax.sharding import PartitionSpec as P

LATENT = 32
RANK = 34
FEAT = 80
BIAS = 3 * FEAT
DEPTH = 256
LANES = 128
ENTROPY = 0.1
LOG2E = 1.4426950408889634
SCALE = LOG2E / ENTROPY

ROW_LOGW = LATENT + RANK
ROW_POT = ROW_LOGW + 1
ROW_RIGHT = 72
PACK = 112
RIGHT = 48
MOMENT = 40
CHUNK = 256
HEADROOM = 100.0
SMALLEST = 2.0**-99
LARGEST = 2.0**126

f32 = jnp.float32
bf16 = jnp.bfloat16


def dot(a, b):
    return jnp.dot(a, b, preferred_element_type=f32)


def dot_nt(a, b):
    return lax.dot_general(a, b, (((1,), (1,)), ((), ())), preferred_element_type=f32)


def split(x):
    hi = x.astype(bf16)
    return hi, (x - hi.astype(f32)).astype(bf16)


def iota(shape, axis):
    return lax.broadcasted_iota(jnp.int32, shape, axis)


def eye():
    shape = (LANES, LANES)
    return iota(shape, 0) == iota(shape, 1)


def to_lanes(column, mask):
    return jnp.sum(jnp.where(mask, column, 0.0), axis=0, keepdims=True)


def tile(t):
    return slice(t * LANES, (t + 1) * LANES)


def features(block):
    x = block[0:FEAT]
    return jnp.where(iota(x.shape, 0) < LATENT + RANK, x, 0.0)


def pick(x, row, n):
    return jnp.concatenate([x[t, row : row + 1, :] for t in range(n)], axis=0)


def half_square(block):
    x = block[0:LATENT]
    return 0.5 * jnp.sum(x * x, axis=0, keepdims=True)


def three(x):
    hi = x.astype(bf16).astype(f32)
    rest = x - hi
    mid = rest.astype(bf16).astype(f32)
    return hi, mid, rest - mid


def extra(terms):
    rows = iota((DEPTH - BIAS, LANES), 0)
    out = jnp.zeros(rows.shape, f32)
    for k, x in terms.items():
        out = jnp.where(rows == k, x, out)
    return out.astype(bf16)


ONES = {0: 1.0, 1: 1.0, 2: 1.0}


def put_bias(ref, potential, more={}):
    for t in range(potential.shape[0]):
        ref[BIAS:DEPTH, tile(t)] = extra(dict(enumerate(three(potential[t : t + 1]))) | more)


def shifted(shift):
    return extra(ONES | {3 + k: x for k, x in enumerate(three(shift))})


def left_operand(xh, xl, moment):
    shape = (LANES, LANES)
    row, column = iota(shape, 0), iota(shape, 1)
    mixed = moment.T + jnp.where((row == column) & (row < LATENT), 1.0, 0.0)
    qh, ql = split((SCALE * mixed)[0:FEAT, 0:FEAT])
    both = dot(jnp.concatenate([qh, ql], axis=0), xh)
    return split(both[0:FEAT] + both[FEAT:] + dot(qh, xl))


def transpose_into(ref, t, block):
    unit = jnp.where(eye(), 1.0, 0.0).astype(bf16)
    ref[tile(t), :] = dot_nt(unit, block).astype(bf16)


def restream(ref, t, fixed, shift):
    unit = jnp.where(eye(), 1.0, 0.0).astype(bf16)
    block = jnp.concatenate([fixed[LANES:BIAS, tile(t)], shifted(shift)], axis=0)
    ref[tile(t), LANES:DEPTH] = dot_nt(unit, block).astype(bf16)


def reduce_rows(s, row, mask):
    tops, totals = [], []
    for k in range(0, LANES, 8):
        x = [s[row + k : row + k + 8, tile(t)] for t in range(s.shape[1] // LANES)]
        top = functools.reduce(jnp.maximum, x)
        tops.append(top)
        totals.append(functools.reduce(jnp.add, [jnp.exp2(y - top) for y in x]))
    top, total = jnp.concatenate(tops, axis=0), jnp.concatenate(totals, axis=0)
    whole = jnp.max(top, axis=1, keepdims=True)
    total = jnp.sum(total * jnp.exp2(top - whole), axis=1, keepdims=True)
    return to_lanes(whole, mask), to_lanes(total, mask)


def add_rows(s, row, mask):
    totals = []
    for k in range(0, LANES, 8):
        x = [jnp.exp2(s[row + k : row + k + 8, tile(t)]) for t in range(s.shape[1] // LANES)]
        totals.append(functools.reduce(jnp.add, x))
    return to_lanes(jnp.sum(jnp.concatenate(totals, axis=0), axis=1, keepdims=True), mask)


def pipeline(stream, fixed, s0, s1, reduce):
    s = (s0, s1)
    steps = stream.shape[0] // CHUNK
    s0[...] = dot(stream[0:CHUNK, :], fixed[...])
    for b in range(steps):
        if b + 1 < steps:
            s[(b + 1) % 2][...] = dot(stream[(b + 1) * CHUNK : (b + 2) * CHUNK, :], fixed[...])
        for k in range(CHUNK // LANES):
            reduce(b * (CHUNK // LANES) + k, s[b % 2], k * LANES)


def lse_rows(stream, fixed, out_ref, own_ref, s0, s1, tops, totals):
    mask = eye()

    def reduce(t, s, row):
        tops[t : t + 1, :], totals[t : t + 1, :] = reduce_rows(s, row, mask)

    pipeline(stream, fixed, s0, s1, reduce)
    write(tops[...] + jnp.log2(totals[...]), out_ref, own_ref)


def write(x, *refs):
    for ref in refs:
        if len(ref.shape) == 2:
            ref[...] = x
        else:
            for k in range(ref.shape[0]):
                ref[k] = x


def shifted_lse_rows(stream, fixed, shift, s0, s1, tops, totals, *refs):
    mask = eye()

    def reduce(t, s, row):
        totals[t : t + 1, :] = add_rows(s, row, mask)

    pipeline(stream, fixed, s0, s1, reduce)
    total = totals[...]
    tops[...] = jnp.log2(total)

    def good(total):
        return jnp.all((total >= SMALLEST) & (total <= LARGEST))

    @pl.when(jnp.logical_not(good(total)))
    def _():
        def step(t, carry):
            @pl.when(jnp.logical_not(good(totals[pl.ds(t, 1), :])))
            def _():
                s0[0:LANES, :] = dot(stream[pl.ds(pl.multiple_of(t * LANES, LANES), LANES), :], fixed[...])
                top, total = reduce_rows(s0, 0, mask)
                tops[pl.ds(t, 1), :] = top + jnp.log2(total)

            return carry

        lax.fori_loop(0, stream.shape[0] // LANES, step, 0)

    write(tops[...] - shift, *refs)


def combine(parts):
    top = jnp.max(parts, axis=0)
    return top + jnp.log2(jnp.sum(jnp.exp2(parts - top[None]), axis=0))


def pack_kernel(n, *refs):
    (source, target), held, sems = refs[9:11], refs[11:20], refs[20]
    copies = [pltpu.make_async_copy(refs[k], held[k], sems.at[k]) for k in range(9)]
    for copy in copies:
        copy.start()
    for copy in copies:
        copy.wait()
    u, a1, b1, la, v, a2, b2, lb, g = held

    def rows(latent, left, right, logw, pot):
        zero = jnp.zeros((ROW_RIGHT - ROW_POT - 1, LANES), f32)
        fill = jnp.zeros((PACK - ROW_RIGHT - RANK, LANES), f32)
        return jnp.concatenate([latent, left, logw, pot, zero, right, fill], axis=0)

    x = rows(u[...], a1[...], b1[...], la[...], jnp.zeros((1, LANES), f32))
    for k in range(n):
        source[k] = x
    target[...] = rows(v[...], a2[:, 0, :], b2[:, 0, :], lb[...], g[...])


def old_kernel(n, blocks, sg, tg, moment, lse_out, lse_own, carried, xh, xl, rt, rc, lt, b2, s0, s1, ph, pl_, held):
    for t in range(blocks):
        hi, low = split(features(tg[t]))
        rt[0:FEAT, tile(t)] = hi
        rt[FEAT : 2 * FEAT, tile(t)] = low
        rt[2 * FEAT : BIAS, tile(t)] = hi
        pot = SCALE * (tg[t, ROW_POT : ROW_POT + 1, :] - half_square(tg[t]))
        transpose_into(rc, t, jnp.concatenate([hi, low, hi, shifted(pot)], axis=0))
        right = jnp.concatenate([tg[t, ROW_RIGHT:PACK, :], jnp.zeros((RIGHT + ROW_RIGHT - PACK, LANES), f32)], axis=0)
        hi, low = split(right)
        b2[0:RIGHT, tile(t)] = hi
        b2[RIGHT:, tile(t)] = low
        hi, low = split(features(sg[t]))
        xh[:, tile(t)] = hi
        xl[:, tile(t)] = low
        lt[BIAS:DEPTH, tile(t)] = extra({3: 1.0, 4: 1.0, 5: 1.0})
    lh, ll = left_operand(xh[...], xl[...], moment[...])
    lt[0:FEAT, :] = lh
    lt[FEAT : 2 * FEAT, :] = lh
    lt[2 * FEAT : BIAS, :] = ll
    cells, piece = rc.shape[0], 64
    steps = lt.shape[1] // CHUNK

    def columns(b):
        return pl.ds(pl.multiple_of(b * CHUNK, CHUNK), CHUNK)

    def scores(b, s):
        s[...] = dot(rc[...], lt[:, columns(b)])

    def plan(b, s):
        top = s[0:piece, :]
        for k in range(piece, cells, piece):
            top = jnp.maximum(top, s[k : k + piece, :])
        top = jnp.max(top, axis=0, keepdims=True)
        total = jnp.zeros((piece, CHUNK), f32)
        for k in range(0, cells, piece):
            p = jnp.exp2(s[k : k + piece, :] - top)
            total = total + p
            hi, low = split(p)
            ph[k : k + piece, :] = hi
            pl_[k : k + piece, :] = low
        total = jnp.sum(total, axis=0, keepdims=True)
        c = dot(b2[...], ph[...])
        c = c[0:RIGHT] + c[RIGHT:] + dot(b2[0:RIGHT, :], pl_[...])
        carried[:, columns(b)] = c / total
        held[:, columns(b)] = top + jnp.log2(total)

    scores(0, s0)

    def step(i, carry):
        scores(2 * i + 1, s1)
        plan(2 * i, s0)
        scores(lax.rem(2 * i + 2, steps), s0)
        plan(2 * i + 1, s1)
        return carry

    lax.fori_loop(0, steps // 2, step, 0)
    lse = jnp.concatenate([held[:, tile(t)] for t in range(cells // LANES)], axis=0)
    lse_own[...] = lse
    for k in range(n):
        lse_out[k] = lse


def moment_kernel(n, blocks, parts, lse_own, carried, sg, f_out, moment_out):
    f = LOG2E * pick(sg, ROW_LOGW, blocks) - combine(parts[...])
    f_out[...] = f
    weight = jnp.exp2(f + lse_own[...])
    left = [sg[t, ROW_RIGHT:PACK, :] * weight[t : t + 1] for t in range(blocks)]
    hi, low = split(jnp.concatenate(left, axis=1))
    ch, cl = split(carried[...])
    fill = jnp.zeros((LANES - RIGHT, ch.shape[1]), bf16)
    ch, cl = jnp.concatenate([ch, fill], axis=0), jnp.concatenate([cl, fill], axis=0)
    x = dot_nt(hi, ch) + dot_nt(low, ch) + dot_nt(hi, cl)
    second, third = pltpu.roll(x[16:32], MOMENT, 1), pltpu.roll(x[32:40], 2 * MOMENT, 1)
    packed = x[0:16] + second + jnp.concatenate([third, jnp.zeros_like(third)], axis=0)
    for k in range(n):
        moment_out[k] = packed


def sum_kernel(n, parts, out):
    total = jnp.sum(parts[...], axis=0)
    for k in range(n):
        out[k] = total


def unpack_moment(packed):
    first = pltpu.roll(packed, LATENT, 1)
    second = pltpu.roll(packed, LANES + LATENT - MOMENT, 1)
    third = pltpu.roll(packed[0:8], LANES + LATENT - 2 * MOMENT, 1)
    x = jnp.concatenate([first, second, third], axis=0)
    rows, lanes = iota(x.shape, 0), iota(x.shape, 1)
    x = jnp.where((rows < RANK) & (lanes >= LATENT) & (lanes < LATENT + RANK), x, 0.0)
    return jnp.concatenate([jnp.zeros((LATENT, LANES), f32), x, jnp.zeros((LANES - LATENT - MOMENT, LANES), f32)], axis=0)


def first_g_kernel(blocks, parts, f, xh, xl, rc, out, own, lc, lt, *scratch):
    moment = unpack_moment(jnp.sum(parts[...], axis=0))
    lh, ll = left_operand(xh[...], xl[...], moment)
    lt[0:FEAT, :] = lh
    lt[FEAT : 2 * FEAT, :] = lh
    lt[2 * FEAT : BIAS, :] = ll
    put_bias(lt, f[...])
    for t in range(blocks):
        more = shifted(f[t : t + 1, :] + HEADROOM)
        transpose_into(lc, t, jnp.concatenate([lt[0:BIAS, tile(t)], more], axis=0))
    lse_rows(rc, lt, out, own, *scratch)


def updated(blocks, parts, gathered):
    return LOG2E * pick(gathered, ROW_LOGW, blocks) - combine(parts[...])


def potential(blocks, x, gathered):
    return x * (1.0 / SCALE) + jnp.concatenate([half_square(gathered[t]) for t in range(blocks)], axis=0)


def half_kernel(blocks, as_shift, parts, gathered, shift, last, stream, fixed_in, other_in, out, own, fixed, other, *scratch):
    x = updated(blocks, parts, gathered)
    put_bias(fixed, x, {3: 1.0, 4: 1.0, 5: 1.0})
    for t in range(blocks):
        restream(other, t, fixed, -last[t : t + 1, :])
    shifted_lse_rows(stream, fixed, as_shift(shift[...]), *scratch, out, own)


def last_half_kernel(blocks, parts, gathered, shift, stream, fixed_in, out, pot_out, fixed, *scratch):
    x = updated(blocks, parts, gathered)
    pot_out[...] = potential(blocks, x, gathered)
    put_bias(fixed, x, {3: 1.0, 4: 1.0, 5: 1.0})
    shifted_lse_rows(stream, fixed, -shift[...], *scratch, out)


def last_kernel(blocks, parts, gathered, pot_out):
    pot_out[...] = potential(blocks, updated(blocks, parts, gathered), gathered)


def call(kernel, out, scratch=(), name=None, aliases={}, space=pltpu.VMEM, semaphores=[], vmem=32):
    spec = pl.BlockSpec(memory_space=pltpu.VMEM)
    return lambda *args: pl.pallas_call(
        kernel,
        out_shape=[jax.ShapeDtypeStruct(s, d) for s, d in out],
        in_specs=[pl.BlockSpec(memory_space=space)] * len(args),
        out_specs=[spec] * len(out),
        scratch_shapes=[pltpu.VMEM(s, d) for s, d in scratch] + semaphores,
        input_output_aliases=aliases,
        compiler_params=pltpu.CompilerParams(vmem_limit_bytes=vmem * 1024 * 1024),
        name=name,
    )(*args)


def swap(x, axis):
    return lax.all_to_all(x, axis, 0, 0)


def shards(n_src, n_tgt, *args):
    (u, a1, b1, la, v, a2, b2, lb, g, old_moment) = args
    v = v.reshape(v.shape[2:])
    a2, b2 = (x.transpose(3, 0, 1, 2).reshape(x.shape[3], 1, -1) for x in (a2, b2))
    flat = lambda x: x.reshape(1, -1)
    cells = (u.T, a1.T, b1.T, flat(la), v.T, a2, b2, flat(lb), flat(g))
    source, target = call(
        functools.partial(pack_kernel, n_tgt),
        [((n_tgt, PACK, LANES), f32), ((PACK, LANES), f32)],
        [(x.shape, f32) for x in cells],
        name="pack",
        space=pltpu.HBM,
        semaphores=[pltpu.SemaphoreType.DMA((len(cells),))],
        vmem=63,
    )(*cells)
    sg = swap(source, "tgt")
    tg = lax.all_gather(target, "src", axis=0)
    bs, bt = n_tgt, n_src
    rows, cols = bs * LANES, bt * LANES
    old = jnp.pad(old_moment, ((LATENT, LANES - LATENT - RANK),) * 2)

    lse, own, carried, xh, xl, rt, rc = call(
        functools.partial(old_kernel, n_tgt, bs),
        [
            ((n_tgt, bs, LANES), f32),
            ((bs, LANES), f32),
            ((RIGHT, rows), f32),
            ((FEAT, rows), bf16),
            ((FEAT, rows), bf16),
            ((DEPTH, cols), bf16),
            ((cols, DEPTH), bf16),
        ],
        [
            ((DEPTH, rows), bf16),
            ((2 * RIGHT, cols), bf16),
            ((cols, CHUNK), f32),
            ((cols, CHUNK), f32),
            ((cols, CHUNK), bf16),
            ((cols, CHUNK), bf16),
            ((1, rows), f32),
        ],
        name="old_plan",
    )(sg, tg, old)
    f, moment = call(
        functools.partial(moment_kernel, n_tgt, bs),
        [((bs, LANES), f32), ((n_tgt, 16, LANES), f32)],
        name="moment",
    )(swap(lse, "tgt"), own, carried, sg)
    (moment,) = call(functools.partial(sum_kernel, n_src), [((n_src, 16, LANES), f32)], name="moment_sum")(
        swap(moment, "tgt")
    )
    pipe = lambda cells, b: [((CHUNK, cells), f32)] * 2 + [((b, LANES), f32)] * 2
    part, last_g, lc, lt = call(
        functools.partial(first_g_kernel, bs),
        [((n_src, bt, LANES), f32), ((bt, LANES), f32), ((rows, DEPTH), bf16), ((DEPTH, rows), bf16)],
        pipe(rows, bt),
        name="first_g",
    )(swap(moment, "src"), f, xh, xl, rc)
    half = lambda n, fixed, streamed, as_shift, name: call(
        functools.partial(half_kernel, fixed, as_shift),
        [
            ((n, streamed, LANES), f32),
            ((streamed, LANES), f32),
            ((DEPTH, fixed * LANES), bf16),
            ((fixed * LANES, DEPTH), bf16),
        ],
        pipe(fixed * LANES, streamed),
        name=name,
        aliases={5: 2, 6: 3},
    )
    part, last_f, rt, rc = half(n_tgt, bt, bs, lambda x: x + HEADROOM, "first_f")(
        swap(part, "src"), tg, f, last_g, lc, rt, rc
    )
    part, _, lt, lc = half(n_src, bs, bt, lambda x: -x, "second_g")(
        swap(part, "tgt"), sg, last_g, last_f, rc, lt, lc
    )
    part, g, _ = call(
        functools.partial(last_half_kernel, bt),
        [((n_tgt, bs, LANES), f32), ((bt, LANES), f32), ((DEPTH, cols), bf16)],
        pipe(cols, bs),
        name="second_f",
        aliases={4: 2},
    )(swap(part, "src"), tg, last_f, lc, rt)
    (f,) = call(functools.partial(last_kernel, bs), [((bs, LANES), f32)], name="last_f")(swap(part, "tgt"), sg)
    return f.reshape(-1), g.reshape(-1)


def solution(mesh):
    return jax.shard_map(
        functools.partial(shards, mesh.shape["src"], mesh.shape["tgt"]),
        mesh=mesh,
        in_specs=(
            P(("src", "tgt"), None),
            P(("src", "tgt"), None),
            P(("src", "tgt"), None),
            P(("src", "tgt")),
            P("tgt", "src", None, None),
            P("tgt", "src", None, None),
            P("tgt", "src", None, None),
            P("tgt", "src", None),
            P("tgt", "src", None),
            P(),
        ),
        out_specs=(P("src"), P("tgt")),
        check_vma=False,
    )
```

```python
import functools

import jax
import jax.numpy as jnp
from jax import lax
from jax.experimental import pallas as pl
from jax.experimental.pallas import tpu as pltpu
from jax.sharding import PartitionSpec as P

LATENT = 32
RANK = 34
FEAT = 80
BIAS = 3 * FEAT
DEPTH = 256
LANES = 128
ENTROPY = 0.1
LOG2E = 1.4426950408889634
SCALE = LOG2E / ENTROPY

ROW_LOGW = LATENT + RANK
ROW_POT = ROW_LOGW + 1
ROW_RIGHT = 72
PACK = 112
RIGHT = 48
MOMENT = 40
CHUNK = 256
HEADROOM = 100.0
SMALLEST = 2.0**-99
LARGEST = 2.0**126

f32 = jnp.float32
bf16 = jnp.bfloat16


def dot(a, b):
    return jnp.dot(a, b, preferred_element_type=f32)


def dot_nt(a, b):
    return lax.dot_general(a, b, (((1,), (1,)), ((), ())), preferred_element_type=f32)


def split(x):
    hi = x.astype(bf16)
    return hi, (x - hi.astype(f32)).astype(bf16)


def iota(shape, axis):
    return lax.broadcasted_iota(jnp.int32, shape, axis)


def eye():
    shape = (LANES, LANES)
    return iota(shape, 0) == iota(shape, 1)


def to_lanes(column, mask):
    return jnp.sum(jnp.where(mask, column, 0.0), axis=0, keepdims=True)


def tile(t):
    return slice(t * LANES, (t + 1) * LANES)


def features(block):
    x = block[0:FEAT]
    return jnp.where(iota(x.shape, 0) < LATENT + RANK, x, 0.0)


def pick(x, row, n):
    return jnp.concatenate([x[t, row : row + 1, :] for t in range(n)], axis=0)


def half_square(block):
    x = block[0:LATENT]
    return 0.5 * jnp.sum(x * x, axis=0, keepdims=True)


def three(x):
    hi = x.astype(bf16).astype(f32)
    rest = x - hi
    mid = rest.astype(bf16).astype(f32)
    return hi, mid, rest - mid


def extra(terms):
    rows = iota((DEPTH - BIAS, LANES), 0)
    out = jnp.zeros(rows.shape, f32)
    for k, x in terms.items():
        out = jnp.where(rows == k, x, out)
    return out.astype(bf16)


ONES = {0: 1.0, 1: 1.0, 2: 1.0}


def put_bias(ref, potential, more={}):
    for t in range(potential.shape[0]):
        ref[BIAS:DEPTH, tile(t)] = extra(dict(enumerate(three(potential[t : t + 1]))) | more)


def shifted(shift):
    return extra(ONES | {3 + k: x for k, x in enumerate(three(shift))})


def left_operand(xh, xl, moment):
    shape = (LANES, LANES)
    row, column = iota(shape, 0), iota(shape, 1)
    mixed = moment.T + jnp.where((row == column) & (row < LATENT), 1.0, 0.0)
    qh, ql = split((SCALE * mixed)[0:FEAT, 0:FEAT])
    both = dot(jnp.concatenate([qh, ql], axis=0), xh)
    return split(both[0:FEAT] + both[FEAT:] + dot(qh, xl))


def transpose_into(ref, t, block):
    unit = jnp.where(eye(), 1.0, 0.0).astype(bf16)
    ref[tile(t), :] = dot_nt(unit, block).astype(bf16)


def restream(ref, t, fixed, shift):
    unit = jnp.where(eye(), 1.0, 0.0).astype(bf16)
    block = jnp.concatenate([fixed[LANES:BIAS, tile(t)], shifted(shift)], axis=0)
    ref[tile(t), LANES:DEPTH] = dot_nt(unit, block).astype(bf16)


def reduce_rows(s, row, mask):
    tops, totals = [], []
    for k in range(0, LANES, 8):
        x = [s[row + k : row + k + 8, tile(t)] for t in range(s.shape[1] // LANES)]
        top = functools.reduce(jnp.maximum, x)
        tops.append(top)
        totals.append(functools.reduce(jnp.add, [jnp.exp2(y - top) for y in x]))
    top, total = jnp.concatenate(tops, axis=0), jnp.concatenate(totals, axis=0)
    whole = jnp.max(top, axis=1, keepdims=True)
    total = jnp.sum(total * jnp.exp2(top - whole), axis=1, keepdims=True)
    return to_lanes(whole, mask), to_lanes(total, mask)


def add_rows(s, row, mask):
    totals = []
    for k in range(0, LANES, 8):
        x = [jnp.exp2(s[row + k : row + k + 8, tile(t)]) for t in range(s.shape[1] // LANES)]
        totals.append(functools.reduce(jnp.add, x))
    return to_lanes(jnp.sum(jnp.concatenate(totals, axis=0), axis=1, keepdims=True), mask)


def pipeline(stream, fixed, s0, s1, reduce):
    s = (s0, s1)
    steps = stream.shape[0] // CHUNK
    s0[...] = dot(stream[0:CHUNK, :], fixed[...])
    for b in range(steps):
        if b + 1 < steps:
            s[(b + 1) % 2][...] = dot(stream[(b + 1) * CHUNK : (b + 2) * CHUNK, :], fixed[...])
        for k in range(CHUNK // LANES):
            reduce(b * (CHUNK // LANES) + k, s[b % 2], k * LANES)


def lse_rows(stream, fixed, out_ref, own_ref, s0, s1, tops, totals):
    mask = eye()

    def reduce(t, s, row):
        tops[t : t + 1, :], totals[t : t + 1, :] = reduce_rows(s, row, mask)

    pipeline(stream, fixed, s0, s1, reduce)
    write(tops[...] + jnp.log2(totals[...]), out_ref, own_ref)


def write(x, *refs):
    for ref in refs:
        if len(ref.shape) == 2:
            ref[...] = x
        else:
            for k in range(ref.shape[0]):
                ref[k] = x


def shifted_lse_rows(stream, fixed, shift, s0, s1, tops, totals, *refs):
    mask = eye()

    def reduce(t, s, row):
        totals[t : t + 1, :] = add_rows(s, row, mask)

    pipeline(stream, fixed, s0, s1, reduce)
    total = totals[...]
    tops[...] = jnp.log2(total)

    def good(total):
        return jnp.all((total >= SMALLEST) & (total <= LARGEST))

    @pl.when(jnp.logical_not(good(total)))
    def _():
        def step(t, carry):
            @pl.when(jnp.logical_not(good(totals[pl.ds(t, 1), :])))
            def _():
                s0[0:LANES, :] = dot(stream[pl.ds(pl.multiple_of(t * LANES, LANES), LANES), :], fixed[...])
                top, total = reduce_rows(s0, 0, mask)
                tops[pl.ds(t, 1), :] = top + jnp.log2(total)

            return carry

        lax.fori_loop(0, stream.shape[0] // LANES, step, 0)

    write(tops[...] - shift, *refs)


def combine(parts):
    top = jnp.max(parts, axis=0)
    return top + jnp.log2(jnp.sum(jnp.exp2(parts - top[None]), axis=0))


def pack_kernel(n, *refs):
    (source, target), held, sems = refs[9:11], refs[11:20], refs[20]
    copies = [pltpu.make_async_copy(refs[k], held[k], sems.at[k]) for k in range(9)]
    for copy in copies:
        copy.start()
    for copy in copies:
        copy.wait()
    u, a1, b1, la, v, a2, b2, lb, g = held

    def rows(latent, left, right, logw, pot):
        zero = jnp.zeros((ROW_RIGHT - ROW_POT - 1, LANES), f32)
        fill = jnp.zeros((PACK - ROW_RIGHT - RANK, LANES), f32)
        return jnp.concatenate([latent, left, logw, pot, zero, right, fill], axis=0)

    x = rows(u[...], a1[...], b1[...], la[...], jnp.zeros((1, LANES), f32))
    for k in range(n):
        source[k] = x
    target[...] = rows(v[...], a2[:, 0, :], b2[:, 0, :], lb[...], g[...])


def old_kernel(n, blocks, sg, tg, moment, lse_out, lse_own, carried, xh, xl, rt, rc, lt, b2, s0, s1, ph, pl_, held):
    for t in range(blocks):
        hi, low = split(features(tg[t]))
        rt[0:FEAT, tile(t)] = hi
        rt[FEAT : 2 * FEAT, tile(t)] = low
        rt[2 * FEAT : BIAS, tile(t)] = hi
        pot = SCALE * (tg[t, ROW_POT : ROW_POT + 1, :] - half_square(tg[t]))
        transpose_into(rc, t, jnp.concatenate([hi, low, hi, shifted(pot)], axis=0))
        right = jnp.concatenate([tg[t, ROW_RIGHT:PACK, :], jnp.zeros((RIGHT + ROW_RIGHT - PACK, LANES), f32)], axis=0)
        right = jnp.where(iota(right.shape, 0) == RANK, 1.0, right)
        hi, low = split(right)
        b2[0:RIGHT, tile(t)] = hi
        b2[RIGHT:, tile(t)] = low
        hi, low = split(features(sg[t]))
        xh[:, tile(t)] = hi
        xl[:, tile(t)] = low
        lt[BIAS:DEPTH, tile(t)] = extra({3: 1.0, 4: 1.0, 5: 1.0})
    lh, ll = left_operand(xh[...], xl[...], moment[...])
    lt[0:FEAT, :] = lh
    lt[FEAT : 2 * FEAT, :] = lh
    lt[2 * FEAT : BIAS, :] = ll
    cells, piece = rc.shape[0], 64
    steps = lt.shape[1] // CHUNK

    def columns(b):
        return pl.ds(pl.multiple_of(b * CHUNK, CHUNK), CHUNK)

    def scores(b, s):
        s[...] = dot(rc[...], lt[:, columns(b)])

    def plan(b, s):
        top = s[0:piece, :]
        for k in range(piece, cells, piece):
            top = jnp.maximum(top, s[k : k + piece, :])
        top = jnp.max(top, axis=0, keepdims=True)
        for k in range(0, cells, piece):
            hi, low = split(jnp.exp2(s[k : k + piece, :] - top))
            ph[k : k + piece, :] = hi
            pl_[k : k + piece, :] = low
        c = dot(b2[...], ph[...])
        c = c[0:RIGHT] + c[RIGHT:] + dot(b2[0:RIGHT, :], pl_[...])
        total = c[RANK : RANK + 1]
        carried[:, columns(b)] = c / total
        held[:, columns(b)] = top + jnp.log2(total)

    scores(0, s0)

    def step(i, carry):
        scores(2 * i + 1, s1)
        plan(2 * i, s0)
        scores(lax.rem(2 * i + 2, steps), s0)
        plan(2 * i + 1, s1)
        return carry

    lax.fori_loop(0, steps // 2, step, 0)
    lse = jnp.concatenate([held[:, tile(t)] for t in range(cells // LANES)], axis=0)
    lse_own[...] = lse
    for k in range(n):
        lse_out[k] = lse


def moment_kernel(n, blocks, parts, lse_own, carried, sg, f_out, moment_out):
    f = LOG2E * pick(sg, ROW_LOGW, blocks) - combine(parts[...])
    f_out[...] = f
    weight = jnp.exp2(f + lse_own[...])
    left = [sg[t, ROW_RIGHT:PACK, :] * weight[t : t + 1] for t in range(blocks)]
    hi, low = split(jnp.concatenate(left, axis=1))
    ch, cl = split(carried[...])
    fill = jnp.zeros((LANES - RIGHT, ch.shape[1]), bf16)
    ch, cl = jnp.concatenate([ch, fill], axis=0), jnp.concatenate([cl, fill], axis=0)
    x = dot_nt(hi, ch) + dot_nt(low, ch) + dot_nt(hi, cl)
    second, third = pltpu.roll(x[16:32], MOMENT, 1), pltpu.roll(x[32:40], 2 * MOMENT, 1)
    packed = x[0:16] + second + jnp.concatenate([third, jnp.zeros_like(third)], axis=0)
    for k in range(n):
        moment_out[k] = packed


def sum_kernel(n, parts, out):
    total = jnp.sum(parts[...], axis=0)
    for k in range(n):
        out[k] = total


def unpack_moment(packed):
    first = pltpu.roll(packed, LATENT, 1)
    second = pltpu.roll(packed, LANES + LATENT - MOMENT, 1)
    third = pltpu.roll(packed[0:8], LANES + LATENT - 2 * MOMENT, 1)
    x = jnp.concatenate([first, second, third], axis=0)
    rows, lanes = iota(x.shape, 0), iota(x.shape, 1)
    x = jnp.where((rows < RANK) & (lanes >= LATENT) & (lanes < LATENT + RANK), x, 0.0)
    return jnp.concatenate([jnp.zeros((LATENT, LANES), f32), x, jnp.zeros((LANES - LATENT - MOMENT, LANES), f32)], axis=0)


def first_g_kernel(blocks, parts, f, xh, xl, rc, out, own, lc, lt, *scratch):
    moment = unpack_moment(jnp.sum(parts[...], axis=0))
    lh, ll = left_operand(xh[...], xl[...], moment)
    lt[0:FEAT, :] = lh
    lt[FEAT : 2 * FEAT, :] = lh
    lt[2 * FEAT : BIAS, :] = ll
    put_bias(lt, f[...])
    for t in range(blocks):
        more = shifted(f[t : t + 1, :] + HEADROOM)
        transpose_into(lc, t, jnp.concatenate([lt[0:BIAS, tile(t)], more], axis=0))
    lse_rows(rc, lt, out, own, *scratch)


def updated(blocks, parts, gathered):
    return LOG2E * pick(gathered, ROW_LOGW, blocks) - combine(parts[...])


def potential(blocks, x, gathered):
    return x * (1.0 / SCALE) + jnp.concatenate([half_square(gathered[t]) for t in range(blocks)], axis=0)


def first_f_kernel(blocks, parts, gathered, f, last, stream, fixed_in, other_in, out, fixed, other, *scratch):
    put_bias(fixed, updated(blocks, parts, gathered), {3: 1.0, 4: 1.0, 5: 1.0})
    for t in range(blocks):
        restream(other, t, fixed, -last[t : t + 1, :])
    shifted_lse_rows(stream, fixed, f[...] + HEADROOM, *scratch, out)


def second_g_kernel(blocks, parts, gathered, last, stream, fixed_in, out, fixed, *scratch):
    put_bias(fixed, updated(blocks, parts, gathered), {3: 1.0, 4: 1.0, 5: 1.0})
    shifted_lse_rows(stream, fixed, -last[...], *scratch, out)


def second_f_kernel(blocks, parts, gathered, f, stream, fixed_in, out, x_out, fixed, *scratch):
    x = updated(blocks, parts, gathered)
    x_out[...] = x
    put_bias(fixed, x, {3: 1.0, 4: 1.0, 5: 1.0})
    shifted_lse_rows(stream, fixed, f[...] + HEADROOM, *scratch, out)


def last_kernel(source_blocks, target_blocks, parts, sg, x, tg, f_out, g_out):
    f_out[...] = potential(source_blocks, updated(source_blocks, parts, sg), sg)
    g_out[...] = potential(target_blocks, x[...], tg)


def call(kernel, out, scratch=(), name=None, aliases={}, space=pltpu.VMEM, semaphores=[], vmem=32):
    spec = pl.BlockSpec(memory_space=pltpu.VMEM)
    return lambda *args: pl.pallas_call(
        kernel,
        out_shape=[jax.ShapeDtypeStruct(s, d) for s, d in out],
        in_specs=[pl.BlockSpec(memory_space=space)] * len(args),
        out_specs=[spec] * len(out),
        scratch_shapes=[pltpu.VMEM(s, d) for s, d in scratch] + semaphores,
        input_output_aliases=aliases,
        compiler_params=pltpu.CompilerParams(vmem_limit_bytes=vmem * 1024 * 1024),
        name=name,
    )(*args)


def swap(x, axis):
    return lax.all_to_all(x, axis, 0, 0)


def shards(n_src, n_tgt, *args):
    (u, a1, b1, la, v, a2, b2, lb, g, old_moment) = args
    v = v.reshape(v.shape[2:])
    a2, b2 = (x.transpose(3, 0, 1, 2).reshape(x.shape[3], 1, -1) for x in (a2, b2))
    flat = lambda x: x.reshape(1, -1)
    cells = (u.T, a1.T, b1.T, flat(la), v.T, a2, b2, flat(lb), flat(g))
    source, target = call(
        functools.partial(pack_kernel, n_tgt),
        [((n_tgt, PACK, LANES), f32), ((PACK, LANES), f32)],
        [(x.shape, f32) for x in cells],
        name="pack",
        space=pltpu.HBM,
        semaphores=[pltpu.SemaphoreType.DMA((len(cells),))],
        vmem=63,
    )(*cells)
    sg = swap(source, "tgt")
    tg = lax.all_gather(target, "src", axis=0)
    bs, bt = n_tgt, n_src
    rows, cols = bs * LANES, bt * LANES
    old = jnp.pad(old_moment, ((LATENT, LANES - LATENT - RANK),) * 2)

    lse, own, carried, xh, xl, rt, rc = call(
        functools.partial(old_kernel, n_tgt, bs),
        [
            ((n_tgt, bs, LANES), f32),
            ((bs, LANES), f32),
            ((RIGHT, rows), f32),
            ((FEAT, rows), bf16),
            ((FEAT, rows), bf16),
            ((DEPTH, cols), bf16),
            ((cols, DEPTH), bf16),
        ],
        [
            ((DEPTH, rows), bf16),
            ((2 * RIGHT, cols), bf16),
            ((cols, CHUNK), f32),
            ((cols, CHUNK), f32),
            ((cols, CHUNK), bf16),
            ((cols, CHUNK), bf16),
            ((1, rows), f32),
        ],
        name="old_plan",
    )(sg, tg, old)
    f, moment = call(
        functools.partial(moment_kernel, n_tgt, bs),
        [((bs, LANES), f32), ((n_tgt, 16, LANES), f32)],
        name="moment",
    )(swap(lse, "tgt"), own, carried, sg)
    (moment,) = call(functools.partial(sum_kernel, n_src), [((n_src, 16, LANES), f32)], name="moment_sum")(
        swap(moment, "tgt")
    )
    pipe = lambda cells, b: [((CHUNK, cells), f32)] * 2 + [((b, LANES), f32)] * 2
    part, last_g, lc, lt = call(
        functools.partial(first_g_kernel, bs),
        [((n_src, bt, LANES), f32), ((bt, LANES), f32), ((rows, DEPTH), bf16), ((DEPTH, rows), bf16)],
        pipe(rows, bt),
        name="first_g",
    )(swap(moment, "src"), f, xh, xl, rc)
    fixed_t, fixed_s, stream_t = ((DEPTH, cols), bf16), ((DEPTH, rows), bf16), ((cols, DEPTH), bf16)
    part, rt, rc = call(
        functools.partial(first_f_kernel, bt),
        [((n_tgt, bs, LANES), f32), fixed_t, stream_t],
        pipe(cols, bs),
        name="first_f",
        aliases={5: 1, 6: 2},
    )(swap(part, "src"), tg, f, last_g, lc, rt, rc)
    part, _ = call(
        functools.partial(second_g_kernel, bs),
        [((n_src, bt, LANES), f32), fixed_s],
        pipe(rows, bt),
        name="second_g",
        aliases={4: 1},
    )(swap(part, "tgt"), sg, last_g, rc, lt)
    part, x, _ = call(
        functools.partial(second_f_kernel, bt),
        [((n_tgt, bs, LANES), f32), ((bt, LANES), f32), fixed_t],
        pipe(cols, bs),
        name="second_f",
        aliases={4: 2},
    )(swap(part, "src"), tg, f, lc, rt)
    f, g = call(
        functools.partial(last_kernel, bs, bt),
        [((bs, LANES), f32), ((bt, LANES), f32)],
        name="last",
    )(swap(part, "tgt"), sg, x, tg)
    return f.reshape(-1), g.reshape(-1)


def solution(mesh):
    return jax.shard_map(
        functools.partial(shards, mesh.shape["src"], mesh.shape["tgt"]),
        mesh=mesh,
        in_specs=(
            P(("src", "tgt"), None),
            P(("src", "tgt"), None),
            P(("src", "tgt"), None),
            P(("src", "tgt")),
            P("tgt", "src", None, None),
            P("tgt", "src", None, None),
            P("tgt", "src", None, None),
            P("tgt", "src", None),
            P("tgt", "src", None),
            P(),
        ),
        out_specs=(P("src"), P("tgt")),
        check_vma=False,
    )
```

```python
import functools

import jax
import jax.numpy as jnp
from jax import lax
from jax.experimental import pallas as pl
from jax.experimental.pallas import tpu as pltpu
from jax.sharding import PartitionSpec as P

LATENT = 32
RANK = 34
FEAT = 80
BIAS = 3 * FEAT
DEPTH = 256
LANES = 128
ENTROPY = 0.1
LOG2E = 1.4426950408889634
SCALE = LOG2E / ENTROPY

ROW_LOGW = LATENT + RANK
ROW_POT = ROW_LOGW + 1
ROW_RIGHT = 72
PACK = 112
RIGHT = 48
MOMENT = 40
CHUNK = 256
HEADROOM = 100.0
SMALLEST = 2.0**-99
LARGEST = 2.0**126

f32 = jnp.float32
bf16 = jnp.bfloat16


def dot(a, b):
    return jnp.dot(a, b, preferred_element_type=f32)


def dot_nt(a, b):
    return lax.dot_general(a, b, (((1,), (1,)), ((), ())), preferred_element_type=f32)


def split(x):
    hi = x.astype(bf16)
    return hi, (x - hi.astype(f32)).astype(bf16)


def iota(shape, axis):
    return lax.broadcasted_iota(jnp.int32, shape, axis)


def eye():
    shape = (LANES, LANES)
    return iota(shape, 0) == iota(shape, 1)


def to_lanes(column, mask):
    return jnp.sum(jnp.where(mask, column, 0.0), axis=0, keepdims=True)


def tile(t):
    return slice(t * LANES, (t + 1) * LANES)


def features(block):
    x = block[0:FEAT]
    return jnp.where(iota(x.shape, 0) < LATENT + RANK, x, 0.0)


def pick(x, row, n):
    return jnp.concatenate([x[t, row : row + 1, :] for t in range(n)], axis=0)


def half_square(block):
    x = block[0:LATENT]
    return 0.5 * jnp.sum(x * x, axis=0, keepdims=True)


def three(x):
    hi = x.astype(bf16).astype(f32)
    rest = x - hi
    mid = rest.astype(bf16).astype(f32)
    return hi, mid, rest - mid


def extra(terms):
    rows = iota((DEPTH - BIAS, LANES), 0)
    out = jnp.zeros(rows.shape, f32)
    for k, x in terms.items():
        out = jnp.where(rows == k, x, out)
    return out.astype(bf16)


ONES = {0: 1.0, 1: 1.0, 2: 1.0}


def put_bias(ref, potential, more={}):
    for t in range(potential.shape[0]):
        ref[BIAS:DEPTH, tile(t)] = extra(dict(enumerate(three(potential[t : t + 1]))) | more)


def shifted(shift):
    return extra(ONES | {3 + k: x for k, x in enumerate(three(shift))})


def left_operand(xh, xl, moment):
    shape = (LANES, LANES)
    row, column = iota(shape, 0), iota(shape, 1)
    mixed = moment.T + jnp.where((row == column) & (row < LATENT), 1.0, 0.0)
    qh, ql = split((SCALE * mixed)[0:FEAT, 0:FEAT])
    both = dot(jnp.concatenate([qh, ql], axis=0), xh)
    return split(both[0:FEAT] + both[FEAT:] + dot(qh, xl))


def transpose_into(ref, t, block):
    unit = jnp.where(eye(), 1.0, 0.0).astype(bf16)
    ref[tile(t), :] = dot_nt(unit, block).astype(bf16)


def restream(ref, t, fixed, shift):
    unit = jnp.where(eye(), 1.0, 0.0).astype(bf16)
    block = jnp.concatenate([fixed[LANES:BIAS, tile(t)], shifted(shift)], axis=0)
    ref[tile(t), LANES:DEPTH] = dot_nt(unit, block).astype(bf16)


def reduce_rows(s, row, mask):
    tops, totals = [], []
    for k in range(0, LANES, 8):
        x = [s[row + k : row + k + 8, tile(t)] for t in range(s.shape[1] // LANES)]
        top = functools.reduce(jnp.maximum, x)
        tops.append(top)
        totals.append(functools.reduce(jnp.add, [jnp.exp2(y - top) for y in x]))
    top, total = jnp.concatenate(tops, axis=0), jnp.concatenate(totals, axis=0)
    whole = jnp.max(top, axis=1, keepdims=True)
    total = jnp.sum(total * jnp.exp2(top - whole), axis=1, keepdims=True)
    return to_lanes(whole, mask), to_lanes(total, mask)


def add_rows(s, row, mask):
    totals = []
    for k in range(0, LANES, 8):
        x = [jnp.exp2(s[row + k : row + k + 8, tile(t)]) for t in range(s.shape[1] // LANES)]
        totals.append(functools.reduce(jnp.add, x))
    return to_lanes(jnp.sum(jnp.concatenate(totals, axis=0), axis=1, keepdims=True), mask)


def pipeline(stream, fixed, s0, s1, reduce, beside):
    s = (s0, s1)
    steps = stream.shape[0] // CHUNK
    s0[...] = dot(stream[0:CHUNK, :], fixed[...])
    for b in range(steps):
        if b + 1 < steps:
            s[(b + 1) % 2][...] = dot(stream[(b + 1) * CHUNK : (b + 2) * CHUNK, :], fixed[...])
        for k in range(CHUNK // LANES):
            beside(b * (CHUNK // LANES) + k)
            reduce(b * (CHUNK // LANES) + k, s[b % 2], k * LANES)


def lse_rows(beside, stream, fixed, out_ref, own_ref, s0, s1, tops, totals):
    mask = eye()

    def reduce(t, s, row):
        tops[t : t + 1, :], totals[t : t + 1, :] = reduce_rows(s, row, mask)

    pipeline(stream, fixed, s0, s1, reduce, beside)
    write(tops[...] + jnp.log2(totals[...]), out_ref, own_ref)


def write(x, *refs):
    for ref in refs:
        if len(ref.shape) == 2:
            ref[...] = x
        else:
            for k in range(ref.shape[0]):
                ref[k] = x


def shifted_lse_rows(beside, stream, fixed, shift, s0, s1, tops, totals, *refs):
    mask = eye()

    def reduce(t, s, row):
        totals[t : t + 1, :] = add_rows(s, row, mask)

    pipeline(stream, fixed, s0, s1, reduce, beside)
    total = totals[...]
    tops[...] = jnp.log2(total)

    def good(total):
        return jnp.all((total >= SMALLEST) & (total <= LARGEST))

    @pl.when(jnp.logical_not(good(total)))
    def _():
        def step(t, carry):
            @pl.when(jnp.logical_not(good(totals[pl.ds(t, 1), :])))
            def _():
                s0[0:LANES, :] = dot(stream[pl.ds(pl.multiple_of(t * LANES, LANES), LANES), :], fixed[...])
                top, total = reduce_rows(s0, 0, mask)
                tops[pl.ds(t, 1), :] = top + jnp.log2(total)

            return carry

        lax.fori_loop(0, stream.shape[0] // LANES, step, 0)

    write(tops[...] - shift, *refs)


def nothing(t):
    pass


def combine(parts):
    top = jnp.max(parts, axis=0)
    return top + jnp.log2(jnp.sum(jnp.exp2(parts - top[None]), axis=0))


def pack_kernel(n, *refs):
    (source, target), held, sems = refs[9:11], refs[11:20], refs[20]
    copies = [pltpu.make_async_copy(refs[k], held[k], sems.at[k]) for k in range(9)]
    for copy in copies:
        copy.start()
    for copy in copies:
        copy.wait()
    u, a1, b1, la, v, a2, b2, lb, g = held

    def rows(latent, left, right, logw, pot):
        zero = jnp.zeros((ROW_RIGHT - ROW_POT - 1, LANES), f32)
        fill = jnp.zeros((PACK - ROW_RIGHT - RANK, LANES), f32)
        return jnp.concatenate([latent, left, logw, pot, zero, right, fill], axis=0)

    x = rows(u[...], a1[...], b1[...], la[...], jnp.zeros((1, LANES), f32))
    for k in range(n):
        source[k] = x
    target[...] = rows(v[...], a2[:, 0, :], b2[:, 0, :], lb[...], g[...])


def old_kernel(n, blocks, sg, tg, moment, lse_out, lse_own, carried, xh, xl, rt, rc, lt, b2, s0, s1, ph0, pl0, ph1, pl1, held):
    for t in range(blocks):
        hi, low = split(features(tg[t]))
        rt[0:FEAT, tile(t)] = hi
        rt[FEAT : 2 * FEAT, tile(t)] = low
        rt[2 * FEAT : BIAS, tile(t)] = hi
        pot = SCALE * (tg[t, ROW_POT : ROW_POT + 1, :] - half_square(tg[t]))
        transpose_into(rc, t, jnp.concatenate([hi, low, hi, shifted(pot)], axis=0))
        hi, low = split(features(sg[t]))
        xh[:, tile(t)] = hi
        xl[:, tile(t)] = low
        lt[BIAS:DEPTH, tile(t)] = extra({3: 1.0, 4: 1.0, 5: 1.0})
    lh, ll = left_operand(xh[...], xl[...], moment[...])
    lt[0:FEAT, :] = lh
    lt[FEAT : 2 * FEAT, :] = lh
    lt[2 * FEAT : BIAS, :] = ll
    cells, piece = rc.shape[0], 64
    steps = lt.shape[1] // CHUNK

    s, p = (s0, s1), ((ph0, pl0), (ph1, pl1))

    def columns(b):
        return slice(b * CHUNK, (b + 1) * CHUNK)

    def scores(b):
        s[b % 2][...] = dot(rc[...], lt[:, columns(b)])

    def exponentials(b):
        x, (high, rest) = s[b % 2], p[b % 2]
        top = x[0:piece, :]
        for k in range(piece, cells, piece):
            top = jnp.maximum(top, x[k : k + piece, :])
        top = jnp.max(top, axis=0, keepdims=True)
        for k in range(0, cells, piece):
            high[k : k + piece, :], rest[k : k + piece, :] = split(jnp.exp2(x[k : k + piece, :] - top))
        held[:, columns(b)] = top

    def carry(b):
        high, rest = p[b % 2]
        c = dot(b2[...], high[...])
        c = c[0:RIGHT] + c[RIGHT:] + dot(b2[0:RIGHT, :], rest[...])
        total = c[RANK : RANK + 1]
        carried[:, columns(b)] = c / total
        held[:, columns(b)] = held[:, columns(b)] + jnp.log2(total)

    scores(0)
    for t in range(blocks):
        right = jnp.concatenate([tg[t, ROW_RIGHT:PACK, :], jnp.zeros((RIGHT + ROW_RIGHT - PACK, LANES), f32)], axis=0)
        right = jnp.where(iota(right.shape, 0) == RANK, 1.0, right)
        b2[0:RIGHT, tile(t)], b2[RIGHT:, tile(t)] = split(right)
    for b in range(steps):
        if b + 1 < steps:
            scores(b + 1)
        exponentials(b)
        if b:
            carry(b - 1)
    carry(steps - 1)
    lse = jnp.concatenate([held[:, tile(t)] for t in range(cells // LANES)], axis=0)
    lse_own[...] = lse
    for k in range(n):
        lse_out[k] = lse


def moment_kernel(n, blocks, parts, lse_own, carried, sg, f_out, moment_out):
    f = LOG2E * pick(sg, ROW_LOGW, blocks) - combine(parts[...])
    f_out[...] = f
    weight = jnp.exp2(f + lse_own[...])
    left = [sg[t, ROW_RIGHT:PACK, :] * weight[t : t + 1] for t in range(blocks)]
    hi, low = split(jnp.concatenate(left, axis=1))
    ch, cl = split(carried[...])
    fill = jnp.zeros((LANES - RIGHT, ch.shape[1]), bf16)
    ch, cl = jnp.concatenate([ch, fill], axis=0), jnp.concatenate([cl, fill], axis=0)
    x = dot_nt(hi, ch) + dot_nt(low, ch) + dot_nt(hi, cl)
    second, third = pltpu.roll(x[16:32], MOMENT, 1), pltpu.roll(x[32:40], 2 * MOMENT, 1)
    packed = x[0:16] + second + jnp.concatenate([third, jnp.zeros_like(third)], axis=0)
    for k in range(n):
        moment_out[k] = packed


def sum_kernel(n, parts, out):
    total = jnp.sum(parts[...], axis=0)
    for k in range(n):
        out[k] = total


def unpack_moment(packed):
    first = pltpu.roll(packed, LATENT, 1)
    second = pltpu.roll(packed, LANES + LATENT - MOMENT, 1)
    third = pltpu.roll(packed[0:8], LANES + LATENT - 2 * MOMENT, 1)
    x = jnp.concatenate([first, second, third], axis=0)
    rows, lanes = iota(x.shape, 0), iota(x.shape, 1)
    x = jnp.where((rows < RANK) & (lanes >= LATENT) & (lanes < LATENT + RANK), x, 0.0)
    return jnp.concatenate([jnp.zeros((LATENT, LANES), f32), x, jnp.zeros((LANES - LATENT - MOMENT, LANES), f32)], axis=0)


def first_g_kernel(blocks, parts, f, xh, xl, rc, out, own, lc, lt, *scratch):
    moment = unpack_moment(jnp.sum(parts[...], axis=0))
    lh, ll = left_operand(xh[...], xl[...], moment)
    lt[0:FEAT, :] = lh
    lt[FEAT : 2 * FEAT, :] = lh
    lt[2 * FEAT : BIAS, :] = ll
    put_bias(lt, f[...])

    def transpose(t):
        if t < blocks:
            more = shifted(f[t : t + 1, :] + HEADROOM)
            transpose_into(lc, t, jnp.concatenate([lt[0:BIAS, tile(t)], more], axis=0))

    for t in range(rc.shape[0] // LANES, blocks):
        transpose(t)
    lse_rows(transpose, rc, lt, out, own, *scratch)


def updated(blocks, parts, gathered):
    return LOG2E * pick(gathered, ROW_LOGW, blocks) - combine(parts[...])


def potential(blocks, x, gathered):
    return x * (1.0 / SCALE) + jnp.concatenate([half_square(gathered[t]) for t in range(blocks)], axis=0)


def first_f_kernel(blocks, parts, gathered, f, last, stream, fixed_in, other_in, out, fixed, other, *scratch):
    put_bias(fixed, updated(blocks, parts, gathered), {3: 1.0, 4: 1.0, 5: 1.0})

    def renew(t):
        if t < blocks:
            restream(other, t, fixed, -last[t : t + 1, :])

    for t in range(stream.shape[0] // LANES, blocks):
        renew(t)
    shifted_lse_rows(renew, stream, fixed, f[...] + HEADROOM, *scratch, out)


def second_g_kernel(blocks, parts, gathered, last, stream, fixed_in, out, fixed, *scratch):
    put_bias(fixed, updated(blocks, parts, gathered), {3: 1.0, 4: 1.0, 5: 1.0})
    shifted_lse_rows(nothing, stream, fixed, -last[...], *scratch, out)


def second_f_kernel(blocks, parts, gathered, f, stream, fixed_in, out, x_out, fixed, *scratch):
    x = updated(blocks, parts, gathered)
    x_out[...] = x
    put_bias(fixed, x, {3: 1.0, 4: 1.0, 5: 1.0})
    shifted_lse_rows(nothing, stream, fixed, f[...] + HEADROOM, *scratch, out)


def last_kernel(source_blocks, target_blocks, parts, sg, x, tg, f_out, g_out):
    f_out[...] = potential(source_blocks, updated(source_blocks, parts, sg), sg)
    g_out[...] = potential(target_blocks, x[...], tg)


def call(kernel, out, scratch=(), name=None, aliases={}, space=pltpu.VMEM, semaphores=[], vmem=32):
    spec = pl.BlockSpec(memory_space=pltpu.VMEM)
    return lambda *args: pl.pallas_call(
        kernel,
        out_shape=[jax.ShapeDtypeStruct(s, d) for s, d in out],
        in_specs=[pl.BlockSpec(memory_space=space)] * len(args),
        out_specs=[spec] * len(out),
        scratch_shapes=[pltpu.VMEM(s, d) for s, d in scratch] + semaphores,
        input_output_aliases=aliases,
        compiler_params=pltpu.CompilerParams(vmem_limit_bytes=vmem * 1024 * 1024),
        name=name,
    )(*args)


def swap(x, axis):
    return lax.all_to_all(x, axis, 0, 0)


def shards(n_src, n_tgt, *args):
    (u, a1, b1, la, v, a2, b2, lb, g, old_moment) = args
    v = v.reshape(v.shape[2:])
    a2, b2 = (x.transpose(3, 0, 1, 2).reshape(x.shape[3], 1, -1) for x in (a2, b2))
    flat = lambda x: x.reshape(1, -1)
    cells = (u.T, a1.T, b1.T, flat(la), v.T, a2, b2, flat(lb), flat(g))
    source, target = call(
        functools.partial(pack_kernel, n_tgt),
        [((n_tgt, PACK, LANES), f32), ((PACK, LANES), f32)],
        [(x.shape, f32) for x in cells],
        name="pack",
        space=pltpu.HBM,
        semaphores=[pltpu.SemaphoreType.DMA((len(cells),))],
        vmem=63,
    )(*cells)
    sg = swap(source, "tgt")
    tg = lax.all_gather(target, "src", axis=0)
    bs, bt = n_tgt, n_src
    rows, cols = bs * LANES, bt * LANES
    old = jnp.pad(old_moment, ((LATENT, LANES - LATENT - RANK),) * 2)

    lse, own, carried, xh, xl, rt, rc = call(
        functools.partial(old_kernel, n_tgt, bs),
        [
            ((n_tgt, bs, LANES), f32),
            ((bs, LANES), f32),
            ((RIGHT, rows), f32),
            ((FEAT, rows), bf16),
            ((FEAT, rows), bf16),
            ((DEPTH, cols), bf16),
            ((cols, DEPTH), bf16),
        ],
        [
            ((DEPTH, rows), bf16),
            ((2 * RIGHT, cols), bf16),
            ((cols, CHUNK), f32),
            ((cols, CHUNK), f32),
            ((cols, CHUNK), bf16),
            ((cols, CHUNK), bf16),
            ((cols, CHUNK), bf16),
            ((cols, CHUNK), bf16),
            ((1, rows), f32),
        ],
        name="old_plan",
    )(sg, tg, old)
    f, moment = call(
        functools.partial(moment_kernel, n_tgt, bs),
        [((bs, LANES), f32), ((n_tgt, 16, LANES), f32)],
        name="moment",
    )(swap(lse, "tgt"), own, carried, sg)
    (moment,) = call(functools.partial(sum_kernel, n_src), [((n_src, 16, LANES), f32)], name="moment_sum")(
        swap(moment, "tgt")
    )
    pipe = lambda cells, b: [((CHUNK, cells), f32)] * 2 + [((b, LANES), f32)] * 2
    part, last_g, lc, lt = call(
        functools.partial(first_g_kernel, bs),
        [((n_src, bt, LANES), f32), ((bt, LANES), f32), ((rows, DEPTH), bf16), ((DEPTH, rows), bf16)],
        pipe(rows, bt),
        name="first_g",
    )(swap(moment, "src"), f, xh, xl, rc)
    fixed_t, fixed_s, stream_t = ((DEPTH, cols), bf16), ((DEPTH, rows), bf16), ((cols, DEPTH), bf16)
    part, rt, rc = call(
        functools.partial(first_f_kernel, bt),
        [((n_tgt, bs, LANES), f32), fixed_t, stream_t],
        pipe(cols, bs),
        name="first_f",
        aliases={5: 1, 6: 2},
    )(swap(part, "src"), tg, f, last_g, lc, rt, rc)
    part, _ = call(
        functools.partial(second_g_kernel, bs),
        [((n_src, bt, LANES), f32), fixed_s],
        pipe(rows, bt),
        name="second_g",
        aliases={4: 1},
    )(swap(part, "tgt"), sg, last_g, rc, lt)
    part, x, _ = call(
        functools.partial(second_f_kernel, bt),
        [((n_tgt, bs, LANES), f32), ((bt, LANES), f32), fixed_t],
        pipe(cols, bs),
        name="second_f",
        aliases={4: 2},
    )(swap(part, "src"), tg, f, lc, rt)
    f, g = call(
        functools.partial(last_kernel, bs, bt),
        [((bs, LANES), f32), ((bt, LANES), f32)],
        name="last",
    )(swap(part, "tgt"), sg, x, tg)
    return f.reshape(-1), g.reshape(-1)


def solution(mesh):
    return jax.shard_map(
        functools.partial(shards, mesh.shape["src"], mesh.shape["tgt"]),
        mesh=mesh,
        in_specs=(
            P(("src", "tgt"), None),
            P(("src", "tgt"), None),
            P(("src", "tgt"), None),
            P(("src", "tgt")),
            P("tgt", "src", None, None),
            P("tgt", "src", None, None),
            P("tgt", "src", None, None),
            P("tgt", "src", None),
            P("tgt", "src", None),
            P(),
        ),
        out_specs=(P("src"), P("tgt")),
        check_vma=False,
    )
```

```python
import functools

import jax
import jax.numpy as jnp
from jax import lax
from jax.experimental import pallas as pl
from jax.experimental.pallas import tpu as pltpu
from jax.sharding import PartitionSpec as P

LATENT = 32
RANK = 34
FEAT = 80
BIAS = 3 * FEAT
DEPTH = 256
LANES = 128
ENTROPY = 0.1
LOG2E = 1.4426950408889634
SCALE = LOG2E / ENTROPY

ROW_LOGW = LATENT + RANK
ROW_POT = ROW_LOGW + 1
ROW_RIGHT = 72
PACK = 112
RIGHT = 48
MOMENT = 40
CHUNK = 256
HEADROOM = 100.0
SMALLEST = 2.0**-99
LARGEST = 2.0**126

f32 = jnp.float32
bf16 = jnp.bfloat16


def dot(a, b):
    return jnp.dot(a, b, preferred_element_type=f32)


def dot_nt(a, b):
    return lax.dot_general(a, b, (((1,), (1,)), ((), ())), preferred_element_type=f32)


def split(x):
    hi = x.astype(bf16)
    return hi, (x - hi.astype(f32)).astype(bf16)


def iota(shape, axis):
    return lax.broadcasted_iota(jnp.int32, shape, axis)


def eye():
    shape = (LANES, LANES)
    return iota(shape, 0) == iota(shape, 1)


def to_lanes(column, mask):
    return jnp.sum(jnp.where(mask, column, 0.0), axis=0, keepdims=True)


def tile(t):
    return slice(t * LANES, (t + 1) * LANES)


def features(block):
    x = block[0:FEAT]
    return jnp.where(iota(x.shape, 0) < LATENT + RANK, x, 0.0)


def pick(x, row, n):
    return jnp.concatenate([x[t, row : row + 1, :] for t in range(n)], axis=0)


def half_square(block):
    x = block[0:LATENT]
    return 0.5 * jnp.sum(x * x, axis=0, keepdims=True)


def three(x):
    hi = x.astype(bf16).astype(f32)
    rest = x - hi
    mid = rest.astype(bf16).astype(f32)
    return hi, mid, rest - mid


def extra(terms):
    rows = iota((DEPTH - BIAS, LANES), 0)
    out = jnp.zeros(rows.shape, f32)
    for k, x in terms.items():
        out = jnp.where(rows == k, x, out)
    return out.astype(bf16)


ONES = {0: 1.0, 1: 1.0, 2: 1.0}


def put_bias(ref, potential, more={}):
    for t in range(potential.shape[0]):
        ref[BIAS:DEPTH, tile(t)] = extra(dict(enumerate(three(potential[t : t + 1]))) | more)


def shifted(shift):
    return extra(ONES | {3 + k: x for k, x in enumerate(three(shift))})


def left_operand(xh, xl, moment):
    shape = (LANES, LANES)
    row, column = iota(shape, 0), iota(shape, 1)
    mixed = moment.T + jnp.where((row == column) & (row < LATENT), 1.0, 0.0)
    qh, ql = split((SCALE * mixed)[0:FEAT, 0:FEAT])
    both = dot(jnp.concatenate([qh, ql], axis=0), xh)
    return split(both[0:FEAT] + both[FEAT:] + dot(qh, xl))


def transpose_into(ref, t, block):
    unit = jnp.where(eye(), 1.0, 0.0).astype(bf16)
    ref[tile(t), :] = dot_nt(unit, block).astype(bf16)


def restream(ref, t, fixed, shift):
    unit = jnp.where(eye(), 1.0, 0.0).astype(bf16)
    block = jnp.concatenate([fixed[LANES:BIAS, tile(t)], shifted(shift)], axis=0)
    ref[tile(t), LANES:DEPTH] = dot_nt(unit, block).astype(bf16)


def reduce_rows(s, row, mask):
    tops, totals = [], []
    for k in range(0, LANES, 8):
        x = [s[row + k : row + k + 8, tile(t)] for t in range(s.shape[1] // LANES)]
        top = functools.reduce(jnp.maximum, x)
        tops.append(top)
        totals.append(functools.reduce(jnp.add, [jnp.exp2(y - top) for y in x]))
    top, total = jnp.concatenate(tops, axis=0), jnp.concatenate(totals, axis=0)
    whole = jnp.max(top, axis=1, keepdims=True)
    total = jnp.sum(total * jnp.exp2(top - whole), axis=1, keepdims=True)
    return to_lanes(whole, mask), to_lanes(total, mask)


def add_rows(s, row, mask):
    totals = []
    for k in range(0, LANES, 8):
        x = [jnp.exp2(s[row + k : row + k + 8, tile(t)]) for t in range(s.shape[1] // LANES)]
        totals.append(functools.reduce(jnp.add, x))
    return to_lanes(jnp.sum(jnp.concatenate(totals, axis=0), axis=1, keepdims=True), mask)


def pipeline(stream, fixed, s0, s1, reduce, beside):
    s = (s0, s1)
    steps = stream.shape[0] // CHUNK
    s0[...] = dot(stream[0:CHUNK, :], fixed[...])
    for b in range(steps):
        if b + 1 < steps:
            s[(b + 1) % 2][...] = dot(stream[(b + 1) * CHUNK : (b + 2) * CHUNK, :], fixed[...])
        for k in range(CHUNK // LANES):
            beside(b * (CHUNK // LANES) + k)
            reduce(b * (CHUNK // LANES) + k, s[b % 2], k * LANES)


def lse_rows(beside, stream, fixed, out_ref, own_ref, s0, s1, tops, totals):
    mask = eye()

    def reduce(t, s, row):
        tops[t : t + 1, :], totals[t : t + 1, :] = reduce_rows(s, row, mask)

    pipeline(stream, fixed, s0, s1, reduce, beside)
    write(tops[...] + jnp.log2(totals[...]), out_ref, own_ref)


def write(x, *refs):
    for ref in refs:
        if len(ref.shape) == 2:
            ref[...] = x
        else:
            for k in range(ref.shape[0]):
                ref[k] = x


def shifted_lse_rows(beside, stream, fixed, shift, s0, s1, tops, totals, *refs):
    mask = eye()

    def reduce(t, s, row):
        totals[t : t + 1, :] = add_rows(s, row, mask)

    pipeline(stream, fixed, s0, s1, reduce, beside)
    total = totals[...]
    tops[...] = jnp.log2(total)

    def good(total):
        return jnp.all((total >= SMALLEST) & (total <= LARGEST))

    @pl.when(jnp.logical_not(good(total)))
    def _():
        def step(t, carry):
            @pl.when(jnp.logical_not(good(totals[pl.ds(t, 1), :])))
            def _():
                s0[0:LANES, :] = dot(stream[pl.ds(pl.multiple_of(t * LANES, LANES), LANES), :], fixed[...])
                top, total = reduce_rows(s0, 0, mask)
                tops[pl.ds(t, 1), :] = top + jnp.log2(total)

            return carry

        lax.fori_loop(0, stream.shape[0] // LANES, step, 0)

    write(tops[...] - shift, *refs)


def nothing(t):
    pass


def combine(parts):
    top = jnp.max(parts, axis=0)
    return top + jnp.log2(jnp.sum(jnp.exp2(parts - top[None]), axis=0))


def pack_kernel(n, *refs):
    (source, target), held, sems = refs[9:11], refs[11:20], refs[20]
    copies = [pltpu.make_async_copy(refs[k], held[k], sems.at[k]) for k in range(9)]
    for copy in copies:
        copy.start()
    for copy in copies:
        copy.wait()
    u, a1, b1, la, v, a2, b2, lb, g = held

    def rows(latent, left, right, logw, pot):
        zero = jnp.zeros((ROW_RIGHT - ROW_POT - 1, LANES), f32)
        fill = jnp.zeros((PACK - ROW_RIGHT - RANK, LANES), f32)
        return jnp.concatenate([latent, left, logw, pot, zero, right, fill], axis=0)

    x = rows(u[...], a1[...], b1[...], la[...], jnp.zeros((1, LANES), f32))
    for k in range(n):
        source[k] = x
    target[...] = rows(v[...], a2[:, 0, :], b2[:, 0, :], lb[...], g[...])


def old_kernel(n, blocks, sg, tg, moment, lse_out, lse_own, carried, xh, xl, rt, rc, lt, b2, s0, s1, ph0, pl0, ph1, pl1, held, padded):
    for t in range(blocks):
        hi, low = split(features(tg[t]))
        rt[0:FEAT, tile(t)] = hi
        rt[FEAT : 2 * FEAT, tile(t)] = low
        rt[2 * FEAT : BIAS, tile(t)] = hi
        pot = SCALE * (tg[t, ROW_POT : ROW_POT + 1, :] - half_square(tg[t]))
        transpose_into(rc, t, jnp.concatenate([hi, low, hi, shifted(pot)], axis=0))
        hi, low = split(features(sg[t]))
        xh[:, tile(t)] = hi
        xl[:, tile(t)] = low
        lt[BIAS:DEPTH, tile(t)] = extra({3: 1.0, 4: 1.0, 5: 1.0})
    used = slice(LATENT, LATENT + RANK)
    padded[...] = jnp.zeros(padded.shape, f32)
    padded[used, used] = moment[...]
    lh, ll = left_operand(xh[...], xl[...], padded[...])
    lt[0:FEAT, :] = lh
    lt[FEAT : 2 * FEAT, :] = lh
    lt[2 * FEAT : BIAS, :] = ll
    cells, piece = rc.shape[0], 64
    steps = lt.shape[1] // CHUNK

    s, p = (s0, s1), ((ph0, pl0), (ph1, pl1))

    def columns(b):
        return slice(b * CHUNK, (b + 1) * CHUNK)

    def scores(b):
        s[b % 2][...] = dot(rc[...], lt[:, columns(b)])

    def exponentials(b):
        x, (high, rest) = s[b % 2], p[b % 2]
        top = x[0:piece, :]
        for k in range(piece, cells, piece):
            top = jnp.maximum(top, x[k : k + piece, :])
        top = jnp.max(top, axis=0, keepdims=True)
        for k in range(0, cells, piece):
            high[k : k + piece, :], rest[k : k + piece, :] = split(jnp.exp2(x[k : k + piece, :] - top))
        held[:, columns(b)] = top

    def carry(b):
        high, rest = p[b % 2]
        c = dot(b2[...], high[...])
        c = c[0:RIGHT] + c[RIGHT:] + dot(b2[0:RIGHT, :], rest[...])
        total = c[RANK : RANK + 1]
        carried[:, columns(b)] = c / total
        held[:, columns(b)] = held[:, columns(b)] + jnp.log2(total)

    scores(0)
    for t in range(blocks):
        right = jnp.concatenate([tg[t, ROW_RIGHT:PACK, :], jnp.zeros((RIGHT + ROW_RIGHT - PACK, LANES), f32)], axis=0)
        right = jnp.where(iota(right.shape, 0) == RANK, 1.0, right)
        b2[0:RIGHT, tile(t)], b2[RIGHT:, tile(t)] = split(right)
    for b in range(steps):
        if b + 1 < steps:
            scores(b + 1)
        exponentials(b)
        if b:
            carry(b - 1)
    carry(steps - 1)
    lse = jnp.concatenate([held[:, tile(t)] for t in range(cells // LANES)], axis=0)
    lse_own[...] = lse
    for k in range(n):
        lse_out[k] = lse


def moment_kernel(n, blocks, parts, lse_own, carried, sg, f_out, moment_out):
    f = LOG2E * pick(sg, ROW_LOGW, blocks) - combine(parts[...])
    f_out[...] = f
    weight = jnp.exp2(f + lse_own[...])
    left = [sg[t, ROW_RIGHT:PACK, :] * weight[t : t + 1] for t in range(blocks)]
    hi, low = split(jnp.concatenate(left, axis=1))
    ch, cl = split(carried[...])
    fill = jnp.zeros((LANES - RIGHT, ch.shape[1]), bf16)
    ch, cl = jnp.concatenate([ch, fill], axis=0), jnp.concatenate([cl, fill], axis=0)
    x = dot_nt(hi, ch) + dot_nt(low, ch) + dot_nt(hi, cl)
    second, third = pltpu.roll(x[16:32], MOMENT, 1), pltpu.roll(x[32:40], 2 * MOMENT, 1)
    packed = x[0:16] + second + jnp.concatenate([third, jnp.zeros_like(third)], axis=0)
    for k in range(n):
        moment_out[k] = packed


def sum_kernel(n, parts, out):
    total = jnp.sum(parts[...], axis=0)
    for k in range(n):
        out[k] = total


def unpack_moment(packed):
    first = pltpu.roll(packed, LATENT, 1)
    second = pltpu.roll(packed, LANES + LATENT - MOMENT, 1)
    third = pltpu.roll(packed[0:8], LANES + LATENT - 2 * MOMENT, 1)
    x = jnp.concatenate([first, second, third], axis=0)
    rows, lanes = iota(x.shape, 0), iota(x.shape, 1)
    x = jnp.where((rows < RANK) & (lanes >= LATENT) & (lanes < LATENT + RANK), x, 0.0)
    return jnp.concatenate([jnp.zeros((LATENT, LANES), f32), x, jnp.zeros((LANES - LATENT - MOMENT, LANES), f32)], axis=0)


def first_g_kernel(blocks, parts, f, xh, xl, rc, out, own, lc, lt, *scratch):
    moment = unpack_moment(jnp.sum(parts[...], axis=0))
    lh, ll = left_operand(xh[...], xl[...], moment)
    lt[0:FEAT, :] = lh
    lt[FEAT : 2 * FEAT, :] = lh
    lt[2 * FEAT : BIAS, :] = ll
    put_bias(lt, f[...])

    def transpose(t):
        if t < blocks:
            more = shifted(f[t : t + 1, :] + HEADROOM)
            transpose_into(lc, t, jnp.concatenate([lt[0:BIAS, tile(t)], more], axis=0))

    for t in range(rc.shape[0] // LANES, blocks):
        transpose(t)
    lse_rows(transpose, rc, lt, out, own, *scratch)


def updated(blocks, parts, gathered):
    return LOG2E * pick(gathered, ROW_LOGW, blocks) - combine(parts[...])


def potential(blocks, x, gathered):
    return x * (1.0 / SCALE) + jnp.concatenate([half_square(gathered[t]) for t in range(blocks)], axis=0)


def first_f_kernel(blocks, parts, gathered, f, last, stream, fixed_in, other_in, out, fixed, other, *scratch):
    put_bias(fixed, updated(blocks, parts, gathered), {3: 1.0, 4: 1.0, 5: 1.0})

    def renew(t):
        if t < blocks:
            restream(other, t, fixed, -last[t : t + 1, :])

    for t in range(stream.shape[0] // LANES, blocks):
        renew(t)
    shifted_lse_rows(renew, stream, fixed, f[...] + HEADROOM, *scratch, out)


def second_g_kernel(blocks, parts, gathered, last, stream, fixed_in, out, fixed, *scratch):
    put_bias(fixed, updated(blocks, parts, gathered), {3: 1.0, 4: 1.0, 5: 1.0})
    shifted_lse_rows(nothing, stream, fixed, -last[...], *scratch, out)


def second_f_kernel(blocks, parts, gathered, f, stream, fixed_in, out, x_out, fixed, *scratch):
    x = updated(blocks, parts, gathered)
    x_out[...] = x
    put_bias(fixed, x, {3: 1.0, 4: 1.0, 5: 1.0})
    shifted_lse_rows(nothing, stream, fixed, f[...] + HEADROOM, *scratch, out)


def last_kernel(source_blocks, target_blocks, parts, sg, x, tg, f_out, g_out):
    f_out[...] = potential(source_blocks, updated(source_blocks, parts, sg), sg)
    g_out[...] = potential(target_blocks, x[...], tg)


def call(kernel, out, scratch=(), name=None, aliases={}, space=pltpu.VMEM, semaphores=[], vmem=32):
    spec = pl.BlockSpec(memory_space=pltpu.VMEM)
    return lambda *args: pl.pallas_call(
        kernel,
        out_shape=[jax.ShapeDtypeStruct(s, d) for s, d in out],
        in_specs=[pl.BlockSpec(memory_space=space)] * len(args),
        out_specs=[spec] * len(out),
        scratch_shapes=[pltpu.VMEM(s, d) for s, d in scratch] + semaphores,
        input_output_aliases=aliases,
        compiler_params=pltpu.CompilerParams(vmem_limit_bytes=vmem * 1024 * 1024),
        name=name,
    )(*args)


def swap(x, axis):
    return lax.all_to_all(x, axis, 0, 0)


def shards(n_src, n_tgt, *args):
    (u, a1, b1, la, v, a2, b2, lb, g, old_moment) = args
    v = v.reshape(v.shape[2:])
    a2, b2 = (x.transpose(3, 0, 1, 2).reshape(x.shape[3], 1, -1) for x in (a2, b2))
    flat = lambda x: x.reshape(1, -1)
    cells = (u.T, a1.T, b1.T, flat(la), v.T, a2, b2, flat(lb), flat(g))
    source, target = call(
        functools.partial(pack_kernel, n_tgt),
        [((n_tgt, PACK, LANES), f32), ((PACK, LANES), f32)],
        [(x.shape, f32) for x in cells],
        name="pack",
        space=pltpu.HBM,
        semaphores=[pltpu.SemaphoreType.DMA((len(cells),))],
        vmem=63,
    )(*cells)
    sg = swap(source, "tgt")
    tg = lax.all_gather(target, "src", axis=0)
    bs, bt = n_tgt, n_src
    rows, cols = bs * LANES, bt * LANES

    lse, own, carried, xh, xl, rt, rc = call(
        functools.partial(old_kernel, n_tgt, bs),
        [
            ((n_tgt, bs, LANES), f32),
            ((bs, LANES), f32),
            ((RIGHT, rows), f32),
            ((FEAT, rows), bf16),
            ((FEAT, rows), bf16),
            ((DEPTH, cols), bf16),
            ((cols, DEPTH), bf16),
        ],
        [
            ((DEPTH, rows), bf16),
            ((2 * RIGHT, cols), bf16),
            ((cols, CHUNK), f32),
            ((cols, CHUNK), f32),
            ((cols, CHUNK), bf16),
            ((cols, CHUNK), bf16),
            ((cols, CHUNK), bf16),
            ((cols, CHUNK), bf16),
            ((1, rows), f32),
            ((LANES, LANES), f32),
        ],
        name="old_plan",
    )(sg, tg, old_moment)
    f, moment = call(
        functools.partial(moment_kernel, n_tgt, bs),
        [((bs, LANES), f32), ((n_tgt, 16, LANES), f32)],
        name="moment",
    )(swap(lse, "tgt"), own, carried, sg)
    (moment,) = call(functools.partial(sum_kernel, n_src), [((n_src, 16, LANES), f32)], name="moment_sum")(
        swap(moment, "tgt")
    )
    pipe = lambda cells, b: [((CHUNK, cells), f32)] * 2 + [((b, LANES), f32)] * 2
    part, last_g, lc, lt = call(
        functools.partial(first_g_kernel, bs),
        [((n_src, bt, LANES), f32), ((bt, LANES), f32), ((rows, DEPTH), bf16), ((DEPTH, rows), bf16)],
        pipe(rows, bt),
        name="first_g",
    )(swap(moment, "src"), f, xh, xl, rc)
    fixed_t, fixed_s, stream_t = ((DEPTH, cols), bf16), ((DEPTH, rows), bf16), ((cols, DEPTH), bf16)
    part, rt, rc = call(
        functools.partial(first_f_kernel, bt),
        [((n_tgt, bs, LANES), f32), fixed_t, stream_t],
        pipe(cols, bs),
        name="first_f",
        aliases={5: 1, 6: 2},
    )(swap(part, "src"), tg, f, last_g, lc, rt, rc)
    part, _ = call(
        functools.partial(second_g_kernel, bs),
        [((n_src, bt, LANES), f32), fixed_s],
        pipe(rows, bt),
        name="second_g",
        aliases={4: 1},
    )(swap(part, "tgt"), sg, last_g, rc, lt)
    part, x, _ = call(
        functools.partial(second_f_kernel, bt),
        [((n_tgt, bs, LANES), f32), ((bt, LANES), f32), fixed_t],
        pipe(cols, bs),
        name="second_f",
        aliases={4: 2},
    )(swap(part, "src"), tg, f, lc, rt)
    f, g = call(
        functools.partial(last_kernel, bs, bt),
        [((bs, LANES), f32), ((bt, LANES), f32)],
        name="last",
    )(swap(part, "tgt"), sg, x, tg)
    return f.reshape(-1), g.reshape(-1)


def solution(mesh):
    return jax.shard_map(
        functools.partial(shards, mesh.shape["src"], mesh.shape["tgt"]),
        mesh=mesh,
        in_specs=(
            P(("src", "tgt"), None),
            P(("src", "tgt"), None),
            P(("src", "tgt"), None),
            P(("src", "tgt")),
            P("tgt", "src", None, None),
            P("tgt", "src", None, None),
            P("tgt", "src", None, None),
            P("tgt", "src", None),
            P("tgt", "src", None),
            P(),
        ),
        out_specs=(P("src"), P("tgt")),
        check_vma=False,
    )
```

```python
import functools

import jax
import jax.numpy as jnp
from jax import lax
from jax.experimental import pallas as pl
from jax.experimental.pallas import tpu as pltpu
from jax.sharding import PartitionSpec as P

LATENT = 32
RANK = 34
FEAT = 80
BIAS = 3 * FEAT
DEPTH = 256
LANES = 128
ENTROPY = 0.1
LOG2E = 1.4426950408889634
SCALE = LOG2E / ENTROPY

ROW_LOGW = LATENT + RANK
ROW_POT = ROW_LOGW + 1
ROW_RIGHT = 72
PACK = 112
RIGHT = 48
MOMENT = 40
CHUNK = 256
HEADROOM = 100.0
SMALLEST = 2.0**-99
LARGEST = 2.0**126

f32 = jnp.float32
bf16 = jnp.bfloat16


def dot(a, b):
    return jnp.dot(a, b, preferred_element_type=f32)


def dot_nt(a, b):
    return lax.dot_general(a, b, (((1,), (1,)), ((), ())), preferred_element_type=f32)


def split(x):
    hi = x.astype(bf16)
    return hi, (x - hi.astype(f32)).astype(bf16)


def iota(shape, axis):
    return lax.broadcasted_iota(jnp.int32, shape, axis)


def eye():
    shape = (LANES, LANES)
    return iota(shape, 0) == iota(shape, 1)


def to_lanes(column, mask):
    return jnp.sum(jnp.where(mask, column, 0.0), axis=0, keepdims=True)


def tile(t):
    return slice(t * LANES, (t + 1) * LANES)


def features(block):
    x = block[0:FEAT]
    return jnp.where(iota(x.shape, 0) < LATENT + RANK, x, 0.0)


def pick(x, row, n):
    return jnp.concatenate([x[t, row : row + 1, :] for t in range(n)], axis=0)


def half_square(block):
    x = block[0:LATENT]
    return 0.5 * jnp.sum(x * x, axis=0, keepdims=True)


def three(x):
    hi = x.astype(bf16).astype(f32)
    rest = x - hi
    mid = rest.astype(bf16).astype(f32)
    return hi, mid, rest - mid


def extra(terms):
    rows = iota((DEPTH - BIAS, LANES), 0)
    out = jnp.zeros(rows.shape, f32)
    for k, x in terms.items():
        out = jnp.where(rows == k, x, out)
    return out.astype(bf16)


ONES = {0: 1.0, 1: 1.0, 2: 1.0}


def put_bias(ref, potential, more={}):
    for t in range(potential.shape[0]):
        ref[BIAS:DEPTH, tile(t)] = extra(dict(enumerate(three(potential[t : t + 1]))) | more)


def shifted(shift):
    return extra(ONES | {3 + k: x for k, x in enumerate(three(shift))})


def left_operand(xh, xl, moment):
    shape = (LANES, LANES)
    row, column = iota(shape, 0), iota(shape, 1)
    mixed = moment.T + jnp.where((row == column) & (row < LATENT), 1.0, 0.0)
    qh, ql = split((SCALE * mixed)[0:FEAT, 0:FEAT])
    both = dot(jnp.concatenate([qh, ql], axis=0), xh)
    return split(both[0:FEAT] + both[FEAT:] + dot(qh, xl))


def transpose_into(ref, t, block):
    unit = jnp.where(eye(), 1.0, 0.0).astype(bf16)
    ref[tile(t), :] = dot_nt(unit, block).astype(bf16)


def restream(ref, t, fixed, shift):
    unit = jnp.where(eye(), 1.0, 0.0).astype(bf16)
    block = jnp.concatenate([fixed[LANES:BIAS, tile(t)], shifted(shift)], axis=0)
    ref[tile(t), LANES:DEPTH] = dot_nt(unit, block).astype(bf16)


def reduce_rows(s, row, mask):
    tops, totals = [], []
    for k in range(0, LANES, 8):
        x = [s[row + k : row + k + 8, tile(t)] for t in range(s.shape[1] // LANES)]
        top = functools.reduce(jnp.maximum, x)
        tops.append(top)
        totals.append(functools.reduce(jnp.add, [jnp.exp2(y - top) for y in x]))
    top, total = jnp.concatenate(tops, axis=0), jnp.concatenate(totals, axis=0)
    whole = jnp.max(top, axis=1, keepdims=True)
    total = jnp.sum(total * jnp.exp2(top - whole), axis=1, keepdims=True)
    return to_lanes(whole, mask), to_lanes(total, mask)


def add_rows(s, row, mask):
    totals = []
    for k in range(0, LANES, 8):
        x = [jnp.exp2(s[row + k : row + k + 8, tile(t)]) for t in range(s.shape[1] // LANES)]
        totals.append(functools.reduce(jnp.add, x))
    return to_lanes(jnp.sum(jnp.concatenate(totals, axis=0), axis=1, keepdims=True), mask)


def pipeline(stream, fixed, s0, s1, reduce, beside):
    s = (s0, s1)
    cells = stream.shape[0]
    edges = [0] + list(range(LANES, cells, CHUNK)) + [cells]
    spans = list(zip(edges[:-1], edges[1:]))

    def multiply(b):
        start, end = spans[b]
        s[b % 2][0 : end - start, :] = dot(stream[start:end, :], fixed[...])

    multiply(0)
    for b, (start, end) in enumerate(spans):
        if b + 1 < len(spans):
            multiply(b + 1)
        for row in range(0, end - start, LANES):
            t = (start + row) // LANES
            beside(t)
            reduce(t, s[b % 2], row)


def lse_rows(beside, stream, fixed, out_ref, own_ref, s0, s1, tops, totals):
    mask = eye()

    def reduce(t, s, row):
        tops[t : t + 1, :], totals[t : t + 1, :] = reduce_rows(s, row, mask)

    pipeline(stream, fixed, s0, s1, reduce, beside)
    write(tops[...] + jnp.log2(totals[...]), out_ref, own_ref)


def write(x, *refs):
    for ref in refs:
        if len(ref.shape) == 2:
            ref[...] = x
        else:
            for k in range(ref.shape[0]):
                ref[k] = x


def shifted_lse_rows(beside, stream, fixed, shift, s0, s1, tops, totals, *refs):
    mask = eye()

    def reduce(t, s, row):
        totals[t : t + 1, :] = add_rows(s, row, mask)

    pipeline(stream, fixed, s0, s1, reduce, beside)
    total = totals[...]
    tops[...] = jnp.log2(total)

    def good(total):
        return jnp.all((total >= SMALLEST) & (total <= LARGEST))

    @pl.when(jnp.logical_not(good(total)))
    def _():
        def step(t, carry):
            @pl.when(jnp.logical_not(good(totals[pl.ds(t, 1), :])))
            def _():
                s0[0:LANES, :] = dot(stream[pl.ds(pl.multiple_of(t * LANES, LANES), LANES), :], fixed[...])
                top, total = reduce_rows(s0, 0, mask)
                tops[pl.ds(t, 1), :] = top + jnp.log2(total)

            return carry

        lax.fori_loop(0, stream.shape[0] // LANES, step, 0)

    write(tops[...] - shift, *refs)


def nothing(t):
    pass


def combine(parts):
    top = jnp.max(parts, axis=0)
    return top + jnp.log2(jnp.sum(jnp.exp2(parts - top[None]), axis=0))


def pack_kernel(n, *refs):
    (source, target), held, sems = refs[9:11], refs[11:20], refs[20]
    copies = [pltpu.make_async_copy(refs[k], held[k], sems.at[k]) for k in range(9)]
    for copy in copies:
        copy.start()
    for copy in copies:
        copy.wait()
    u, a1, b1, la, v, a2, b2, lb, g = held

    def rows(latent, left, right, logw, pot):
        zero = jnp.zeros((ROW_RIGHT - ROW_POT - 1, LANES), f32)
        fill = jnp.zeros((PACK - ROW_RIGHT - RANK, LANES), f32)
        return jnp.concatenate([latent, left, logw, pot, zero, right, fill], axis=0)

    x = rows(u[...], a1[...], b1[...], la[...], jnp.zeros((1, LANES), f32))
    for k in range(n):
        source[k] = x
    target[...] = rows(v[...], a2[:, 0, :], b2[:, 0, :], lb[...], g[...])


def old_kernel(n, blocks, sg, tg, moment, lse_out, lse_own, carried, xh, xl, rt, rc, lt, b2, s0, s1, ph0, pl0, ph1, pl1, held, padded):
    for t in range(blocks):
        hi, low = split(features(tg[t]))
        rt[0:FEAT, tile(t)] = hi
        rt[FEAT : 2 * FEAT, tile(t)] = low
        rt[2 * FEAT : BIAS, tile(t)] = hi
        pot = SCALE * (tg[t, ROW_POT : ROW_POT + 1, :] - half_square(tg[t]))
        transpose_into(rc, t, jnp.concatenate([hi, low, hi, shifted(pot)], axis=0))
        hi, low = split(features(sg[t]))
        xh[:, tile(t)] = hi
        xl[:, tile(t)] = low
        lt[BIAS:DEPTH, tile(t)] = extra({3: 1.0, 4: 1.0, 5: 1.0})
    used = slice(LATENT, LATENT + RANK)
    padded[...] = jnp.zeros(padded.shape, f32)
    padded[used, used] = moment[...]
    lh, ll = left_operand(xh[...], xl[...], padded[...])
    lt[0:FEAT, :] = lh
    lt[FEAT : 2 * FEAT, :] = lh
    lt[2 * FEAT : BIAS, :] = ll
    cells, piece = rc.shape[0], 64
    steps = lt.shape[1] // CHUNK

    s, p = (s0, s1), ((ph0, pl0), (ph1, pl1))

    def columns(b):
        return slice(b * CHUNK, (b + 1) * CHUNK)

    def scores(b):
        s[b % 2][...] = dot(rc[...], lt[:, columns(b)])

    def exponentials(b):
        x, (high, rest) = s[b % 2], p[b % 2]
        top = x[0:piece, :]
        for k in range(piece, cells, piece):
            top = jnp.maximum(top, x[k : k + piece, :])
        top = jnp.max(top, axis=0, keepdims=True)
        for k in range(0, cells, piece):
            high[k : k + piece, :], rest[k : k + piece, :] = split(jnp.exp2(x[k : k + piece, :] - top))
        held[:, columns(b)] = top

    def carry(b):
        high, rest = p[b % 2]
        c = dot(b2[...], high[...])
        c = c[0:RIGHT] + c[RIGHT:] + dot(b2[0:RIGHT, :], rest[...])
        total = c[RANK : RANK + 1]
        carried[:, columns(b)] = c / total
        held[:, columns(b)] = held[:, columns(b)] + jnp.log2(total)

    scores(0)
    for t in range(blocks):
        right = jnp.concatenate([tg[t, ROW_RIGHT:PACK, :], jnp.zeros((RIGHT + ROW_RIGHT - PACK, LANES), f32)], axis=0)
        right = jnp.where(iota(right.shape, 0) == RANK, 1.0, right)
        b2[0:RIGHT, tile(t)], b2[RIGHT:, tile(t)] = split(right)
    for b in range(steps):
        if b + 1 < steps:
            scores(b + 1)
        exponentials(b)
        if b:
            carry(b - 1)
    carry(steps - 1)
    lse = jnp.concatenate([held[:, tile(t)] for t in range(cells // LANES)], axis=0)
    lse_own[...] = lse
    for k in range(n):
        lse_out[k] = lse


def moment_kernel(n, blocks, parts, lse_own, carried, sg, f_out, moment_out):
    f = LOG2E * pick(sg, ROW_LOGW, blocks) - combine(parts[...])
    f_out[...] = f
    weight = jnp.exp2(f + lse_own[...])
    left = [sg[t, ROW_RIGHT:PACK, :] * weight[t : t + 1] for t in range(blocks)]
    hi, low = split(jnp.concatenate(left, axis=1))
    ch, cl = split(carried[...])
    fill = jnp.zeros((LANES - RIGHT, ch.shape[1]), bf16)
    ch, cl = jnp.concatenate([ch, fill], axis=0), jnp.concatenate([cl, fill], axis=0)
    x = dot_nt(hi, ch) + dot_nt(low, ch) + dot_nt(hi, cl)
    packed = x[0:12] + pltpu.roll(x[12:24], MOMENT, 1) + pltpu.roll(x[24:36], 2 * MOMENT, 1)
    for k in range(n):
        moment_out[k, :, 0, :] = packed


def sum_kernel(n, parts, out):
    total = jnp.sum(parts[...], axis=0)
    for k in range(n):
        out[k] = total


def unpack_moment(packed):
    first = pltpu.roll(packed, LATENT, 1)
    second = pltpu.roll(packed, LANES + LATENT - MOMENT, 1)
    third = pltpu.roll(packed, LANES + LATENT - 2 * MOMENT, 1)
    x = jnp.concatenate([first, second, third, jnp.zeros((MOMENT - 36, LANES), f32)], axis=0)
    rows, lanes = iota(x.shape, 0), iota(x.shape, 1)
    x = jnp.where((rows < RANK) & (lanes >= LATENT) & (lanes < LATENT + RANK), x, 0.0)
    return jnp.concatenate([jnp.zeros((LATENT, LANES), f32), x, jnp.zeros((LANES - LATENT - MOMENT, LANES), f32)], axis=0)


def first_g_kernel(blocks, parts, f, xh, xl, rc, out, own, lc, lt, *scratch):
    moment = unpack_moment(jnp.sum(parts[...], axis=0)[:, 0, :])
    lh, ll = left_operand(xh[...], xl[...], moment)
    lt[0:FEAT, :] = lh
    lt[FEAT : 2 * FEAT, :] = lh
    lt[2 * FEAT : BIAS, :] = ll
    put_bias(lt, f[...])

    def transpose(t):
        if t < blocks:
            more = shifted(f[t : t + 1, :] + HEADROOM)
            transpose_into(lc, t, jnp.concatenate([lt[0:BIAS, tile(t)], more], axis=0))

    for t in range(rc.shape[0] // LANES, blocks):
        transpose(t)
    lse_rows(transpose, rc, lt, out, own, *scratch)


def updated(blocks, parts, gathered):
    return LOG2E * pick(gathered, ROW_LOGW, blocks) - combine(parts[...])


def potential(blocks, x, gathered):
    return x * (1.0 / SCALE) + jnp.concatenate([half_square(gathered[t]) for t in range(blocks)], axis=0)


def first_f_kernel(blocks, parts, gathered, f, last, stream, fixed_in, other_in, out, fixed, other, *scratch):
    put_bias(fixed, updated(blocks, parts, gathered), {3: 1.0, 4: 1.0, 5: 1.0})

    def renew(t):
        if t < blocks:
            restream(other, t, fixed, -last[t : t + 1, :])

    for t in range(stream.shape[0] // LANES, blocks):
        renew(t)
    shifted_lse_rows(renew, stream, fixed, f[...] + HEADROOM, *scratch, out)


def second_g_kernel(blocks, parts, gathered, last, stream, fixed_in, out, fixed, *scratch):
    put_bias(fixed, updated(blocks, parts, gathered), {3: 1.0, 4: 1.0, 5: 1.0})
    shifted_lse_rows(nothing, stream, fixed, -last[...], *scratch, out)


def second_f_kernel(blocks, parts, gathered, f, stream, fixed_in, out, x_out, fixed, *scratch):
    x = updated(blocks, parts, gathered)
    x_out[...] = x
    put_bias(fixed, x, {3: 1.0, 4: 1.0, 5: 1.0})
    shifted_lse_rows(nothing, stream, fixed, f[...] + HEADROOM, *scratch, out)


def last_kernel(source_blocks, target_blocks, parts, sg, x, tg, f_out, g_out):
    f_out[...] = potential(source_blocks, updated(source_blocks, parts, sg), sg)
    g_out[...] = potential(target_blocks, x[...], tg)


def call(kernel, out, scratch=(), name=None, aliases={}, space=pltpu.VMEM, semaphores=[], vmem=32):
    spec = pl.BlockSpec(memory_space=pltpu.VMEM)
    return lambda *args: pl.pallas_call(
        kernel,
        out_shape=[jax.ShapeDtypeStruct(s, d) for s, d in out],
        in_specs=[pl.BlockSpec(memory_space=space)] * len(args),
        out_specs=[spec] * len(out),
        scratch_shapes=[pltpu.VMEM(s, d) for s, d in scratch] + semaphores,
        input_output_aliases=aliases,
        compiler_params=pltpu.CompilerParams(vmem_limit_bytes=vmem * 1024 * 1024),
        name=name,
    )(*args)


def swap(x, axis):
    return lax.all_to_all(x, axis, 0, 0)


def shards(n_src, n_tgt, *args):
    (u, a1, b1, la, v, a2, b2, lb, g, old_moment) = args
    v = v.reshape(v.shape[2:])
    a2, b2 = (x.transpose(3, 0, 1, 2).reshape(x.shape[3], 1, -1) for x in (a2, b2))
    flat = lambda x: x.reshape(1, -1)
    cells = (u.T, a1.T, b1.T, flat(la), v.T, a2, b2, flat(lb), flat(g))
    source, target = call(
        functools.partial(pack_kernel, n_tgt),
        [((n_tgt, PACK, LANES), f32), ((PACK, LANES), f32)],
        [(x.shape, f32) for x in cells],
        name="pack",
        space=pltpu.HBM,
        semaphores=[pltpu.SemaphoreType.DMA((len(cells),))],
        vmem=63,
    )(*cells)
    sg = swap(source, "tgt")
    tg = lax.all_gather(target, "src", axis=0)
    bs, bt = n_tgt, n_src
    rows, cols = bs * LANES, bt * LANES

    lse, own, carried, xh, xl, rt, rc = call(
        functools.partial(old_kernel, n_tgt, bs),
        [
            ((n_tgt, bs, LANES), f32),
            ((bs, LANES), f32),
            ((RIGHT, rows), f32),
            ((FEAT, rows), bf16),
            ((FEAT, rows), bf16),
            ((DEPTH, cols), bf16),
            ((cols, DEPTH), bf16),
        ],
        [
            ((DEPTH, rows), bf16),
            ((2 * RIGHT, cols), bf16),
            ((cols, CHUNK), f32),
            ((cols, CHUNK), f32),
            ((cols, CHUNK), bf16),
            ((cols, CHUNK), bf16),
            ((cols, CHUNK), bf16),
            ((cols, CHUNK), bf16),
            ((1, rows), f32),
            ((LANES, LANES), f32),
        ],
        name="old_plan",
    )(sg, tg, old_moment)
    f, moment = call(
        functools.partial(moment_kernel, n_tgt, bs),
        [((bs, LANES), f32), ((n_tgt, 12, 1, LANES), f32)],
        name="moment",
    )(swap(lse, "tgt"), own, carried, sg)
    (moment,) = call(functools.partial(sum_kernel, n_src), [((n_src, 12, 1, LANES), f32)], name="moment_sum")(
        swap(moment, "tgt")
    )
    pipe = lambda cells, b: [((CHUNK, cells), f32)] * 2 + [((b, LANES), f32)] * 2
    part, last_g, lc, lt = call(
        functools.partial(first_g_kernel, bs),
        [((n_src, bt, LANES), f32), ((bt, LANES), f32), ((rows, DEPTH), bf16), ((DEPTH, rows), bf16)],
        pipe(rows, bt),
        name="first_g",
    )(swap(moment, "src"), f, xh, xl, rc)
    fixed_t, fixed_s, stream_t = ((DEPTH, cols), bf16), ((DEPTH, rows), bf16), ((cols, DEPTH), bf16)
    part, rt, rc = call(
        functools.partial(first_f_kernel, bt),
        [((n_tgt, bs, LANES), f32), fixed_t, stream_t],
        pipe(cols, bs),
        name="first_f",
        aliases={5: 1, 6: 2},
    )(swap(part, "src"), tg, f, last_g, lc, rt, rc)
    part, _ = call(
        functools.partial(second_g_kernel, bs),
        [((n_src, bt, LANES), f32), fixed_s],
        pipe(rows, bt),
        name="second_g",
        aliases={4: 1},
    )(swap(part, "tgt"), sg, last_g, rc, lt)
    part, x, _ = call(
        functools.partial(second_f_kernel, bt),
        [((n_tgt, bs, LANES), f32), ((bt, LANES), f32), fixed_t],
        pipe(cols, bs),
        name="second_f",
        aliases={4: 2},
    )(swap(part, "src"), tg, f, lc, rt)
    f, g = call(
        functools.partial(last_kernel, bs, bt),
        [((bs, LANES), f32), ((bt, LANES), f32)],
        name="last",
    )(swap(part, "tgt"), sg, x, tg)
    return f.reshape(-1), g.reshape(-1)


def solution(mesh):
    return jax.shard_map(
        functools.partial(shards, mesh.shape["src"], mesh.shape["tgt"]),
        mesh=mesh,
        in_specs=(
            P(("src", "tgt"), None),
            P(("src", "tgt"), None),
            P(("src", "tgt"), None),
            P(("src", "tgt")),
            P("tgt", "src", None, None),
            P("tgt", "src", None, None),
            P("tgt", "src", None, None),
            P("tgt", "src", None),
            P("tgt", "src", None),
            P(),
        ),
        out_specs=(P("src"), P("tgt")),
        check_vma=False,
    )
```

```python
import functools

import jax
import jax.numpy as jnp
from jax import lax
from jax.experimental import pallas as pl
from jax.experimental.pallas import tpu as pltpu
from jax.sharding import PartitionSpec as P

LATENT = 32
RANK = 34
FEAT = 80
BIAS = 3 * FEAT
DEPTH = 256
LANES = 128
ENTROPY = 0.1
LOG2E = 1.4426950408889634
SCALE = LOG2E / ENTROPY

ROW_LOGW = LATENT + RANK
ROW_POT = ROW_LOGW + 1
ROW_RIGHT = 72
PACK = 112
RIGHT = 48
MOMENT = 40
CHUNK = 256
HEADROOM = 100.0
SMALLEST = 2.0**-99
LARGEST = 2.0**126

f32 = jnp.float32
bf16 = jnp.bfloat16


def dot(a, b):
    return jnp.dot(a, b, preferred_element_type=f32)


def dot_nt(a, b):
    return lax.dot_general(a, b, (((1,), (1,)), ((), ())), preferred_element_type=f32)


def split(x):
    hi = x.astype(bf16)
    return hi, (x - hi.astype(f32)).astype(bf16)


def iota(shape, axis):
    return lax.broadcasted_iota(jnp.int32, shape, axis)


def eye():
    shape = (LANES, LANES)
    return iota(shape, 0) == iota(shape, 1)


def to_lanes(column, mask):
    return jnp.sum(jnp.where(mask, column, 0.0), axis=0, keepdims=True)


def tile(t):
    return slice(t * LANES, (t + 1) * LANES)


def features(block):
    x = block[0:FEAT]
    return jnp.where(iota(x.shape, 0) < LATENT + RANK, x, 0.0)


def pick(x, row, n):
    return jnp.concatenate([x[t, row : row + 1, :] for t in range(n)], axis=0)


def half_square(block):
    x = block[0:LATENT]
    return 0.5 * jnp.sum(x * x, axis=0, keepdims=True)


def three(x):
    hi = x.astype(bf16).astype(f32)
    rest = x - hi
    mid = rest.astype(bf16).astype(f32)
    return hi, mid, rest - mid


def extra(terms):
    rows = iota((DEPTH - BIAS, LANES), 0)
    out = jnp.zeros(rows.shape, f32)
    for k, x in terms.items():
        out = jnp.where(rows == k, x, out)
    return out.astype(bf16)


ONES = {0: 1.0, 1: 1.0, 2: 1.0}


def put_bias(ref, potential, more={}):
    for t in range(potential.shape[0]):
        ref[BIAS:DEPTH, tile(t)] = extra(dict(enumerate(three(potential[t : t + 1]))) | more)


def shifted(shift):
    return extra(ONES | {3 + k: x for k, x in enumerate(three(shift))})


def left_operand(xh, xl, moment):
    shape = (LANES, LANES)
    row, column = iota(shape, 0), iota(shape, 1)
    mixed = moment.T + jnp.where((row == column) & (row < LATENT), 1.0, 0.0)
    qh, ql = split((SCALE * mixed)[0:FEAT, 0:FEAT])
    both = dot(jnp.concatenate([qh, ql], axis=0), xh)
    return split(both[0:FEAT] + both[FEAT:] + dot(qh, xl))


def transpose_into(ref, t, block):
    unit = jnp.where(eye(), 1.0, 0.0).astype(bf16)
    ref[tile(t), :] = dot_nt(unit, block).astype(bf16)


def restream(ref, t, fixed, shift):
    unit = jnp.where(eye(), 1.0, 0.0).astype(bf16)
    block = jnp.concatenate([fixed[LANES:BIAS, tile(t)], shifted(shift)], axis=0)
    ref[tile(t), LANES:DEPTH] = dot_nt(unit, block).astype(bf16)


def reduce_rows(s, row, mask):
    tops, totals = [], []
    for k in range(0, LANES, 8):
        x = [s[row + k : row + k + 8, tile(t)] for t in range(s.shape[1] // LANES)]
        top = functools.reduce(jnp.maximum, x)
        tops.append(top)
        totals.append(functools.reduce(jnp.add, [jnp.exp2(y - top) for y in x]))
    top, total = jnp.concatenate(tops, axis=0), jnp.concatenate(totals, axis=0)
    whole = jnp.max(top, axis=1, keepdims=True)
    total = jnp.sum(total * jnp.exp2(top - whole), axis=1, keepdims=True)
    return to_lanes(whole, mask), to_lanes(total, mask)


def add_rows(s, row, mask):
    totals = []
    for k in range(0, LANES, 8):
        x = [jnp.exp2(s[row + k : row + k + 8, tile(t)]) for t in range(s.shape[1] // LANES)]
        totals.append(functools.reduce(jnp.add, x))
    return to_lanes(jnp.sum(jnp.concatenate(totals, axis=0), axis=1, keepdims=True), mask)


def pipeline(stream, fixed, s0, s1, reduce, beside):
    s = (s0, s1)
    cells = stream.shape[0]
    edges = [0] + list(range(LANES, cells, CHUNK)) + [cells]
    spans = list(zip(edges[:-1], edges[1:]))

    def multiply(b):
        start, end = spans[b]
        s[b % 2][0 : end - start, :] = dot(stream[start:end, :], fixed[...])

    multiply(0)
    for b, (start, end) in enumerate(spans):
        if b + 1 < len(spans):
            multiply(b + 1)
        for row in range(0, end - start, LANES):
            t = (start + row) // LANES
            beside(t)
            reduce(t, s[b % 2], row)


def lse_rows(beside, stream, fixed, out_ref, own_ref, s0, s1, tops, totals):
    mask = eye()

    def reduce(t, s, row):
        tops[t : t + 1, :], totals[t : t + 1, :] = reduce_rows(s, row, mask)

    pipeline(stream, fixed, s0, s1, reduce, beside)
    write(tops[...] + jnp.log2(totals[...]), out_ref, own_ref)


def write(x, *refs):
    for ref in refs:
        if len(ref.shape) == 2:
            ref[...] = x
        else:
            for k in range(ref.shape[0]):
                ref[k, :, 0, :] = x


def shifted_lse_rows(beside, stream, fixed, shift, s0, s1, tops, totals, *refs):
    mask = eye()

    def reduce(t, s, row):
        totals[t : t + 1, :] = add_rows(s, row, mask)

    pipeline(stream, fixed, s0, s1, reduce, beside)
    total = totals[...]
    tops[...] = jnp.log2(total)

    def good(total):
        return jnp.all((total >= SMALLEST) & (total <= LARGEST))

    @pl.when(jnp.logical_not(good(total)))
    def _():
        def step(t, carry):
            @pl.when(jnp.logical_not(good(totals[pl.ds(t, 1), :])))
            def _():
                s0[0:LANES, :] = dot(stream[pl.ds(pl.multiple_of(t * LANES, LANES), LANES), :], fixed[...])
                top, total = reduce_rows(s0, 0, mask)
                tops[pl.ds(t, 1), :] = top + jnp.log2(total)

            return carry

        lax.fori_loop(0, stream.shape[0] // LANES, step, 0)

    write(tops[...] - shift, *refs)


def nothing(t):
    pass


def combine(parts):
    top = jnp.max(parts, axis=0)
    return top + jnp.log2(jnp.sum(jnp.exp2(parts - top[None]), axis=0))


def pack_kernel(n, *refs):
    (source, target), held, sems = refs[9:11], refs[11:20], refs[20]
    copies = [pltpu.make_async_copy(refs[k], held[k], sems.at[k]) for k in range(9)]
    for copy in copies:
        copy.start()
    for copy in copies:
        copy.wait()
    u, a1, b1, la, v, a2, b2, lb, g = held

    def rows(latent, left, right, logw, pot):
        zero = jnp.zeros((ROW_RIGHT - ROW_POT - 1, LANES), f32)
        fill = jnp.zeros((PACK - ROW_RIGHT - RANK, LANES), f32)
        return jnp.concatenate([latent, left, logw, pot, zero, right, fill], axis=0)

    x = rows(u[...], a1[...], b1[...], la[...], jnp.zeros((1, LANES), f32))
    for k in range(n):
        source[k] = x
    target[...] = rows(v[...], a2[:, 0, :], b2[:, 0, :], lb[...], g[...])


def old_kernel(n, blocks, sg, tg, moment, lse_out, lse_own, carried, xh, xl, rt, rc, lt, b2, s0, s1, ph0, pl0, ph1, pl1, held, padded):
    for t in range(blocks):
        hi, low = split(features(tg[t]))
        rt[0:FEAT, tile(t)] = hi
        rt[FEAT : 2 * FEAT, tile(t)] = low
        rt[2 * FEAT : BIAS, tile(t)] = hi
        pot = SCALE * (tg[t, ROW_POT : ROW_POT + 1, :] - half_square(tg[t]))
        transpose_into(rc, t, jnp.concatenate([hi, low, hi, shifted(pot)], axis=0))
        hi, low = split(features(sg[t]))
        xh[:, tile(t)] = hi
        xl[:, tile(t)] = low
        lt[BIAS:DEPTH, tile(t)] = extra({3: 1.0, 4: 1.0, 5: 1.0})
    used = slice(LATENT, LATENT + RANK)
    padded[...] = jnp.zeros(padded.shape, f32)
    padded[used, used] = moment[...]
    lh, ll = left_operand(xh[...], xl[...], padded[...])
    lt[0:FEAT, :] = lh
    lt[FEAT : 2 * FEAT, :] = lh
    lt[2 * FEAT : BIAS, :] = ll
    cells, piece = rc.shape[0], 64
    steps = lt.shape[1] // CHUNK

    s, p = (s0, s1), ((ph0, pl0), (ph1, pl1))

    def columns(b):
        return slice(b * CHUNK, (b + 1) * CHUNK)

    def scores(b):
        s[b % 2][...] = dot(rc[...], lt[:, columns(b)])

    def exponentials(b):
        x, (high, rest) = s[b % 2], p[b % 2]
        top = x[0:piece, :]
        for k in range(piece, cells, piece):
            top = jnp.maximum(top, x[k : k + piece, :])
        top = jnp.max(top, axis=0, keepdims=True)
        for k in range(0, cells, piece):
            high[k : k + piece, :], rest[k : k + piece, :] = split(jnp.exp2(x[k : k + piece, :] - top))
        held[:, columns(b)] = top

    def carry(b):
        high, rest = p[b % 2]
        c = dot(b2[...], high[...])
        c = c[0:RIGHT] + c[RIGHT:] + dot(b2[0:RIGHT, :], rest[...])
        total = c[RANK : RANK + 1]
        carried[:, columns(b)] = c / total
        held[:, columns(b)] = held[:, columns(b)] + jnp.log2(total)

    scores(0)
    for t in range(blocks):
        right = jnp.concatenate([tg[t, ROW_RIGHT:PACK, :], jnp.zeros((RIGHT + ROW_RIGHT - PACK, LANES), f32)], axis=0)
        right = jnp.where(iota(right.shape, 0) == RANK, 1.0, right)
        b2[0:RIGHT, tile(t)], b2[RIGHT:, tile(t)] = split(right)
    for b in range(steps):
        if b + 1 < steps:
            scores(b + 1)
        exponentials(b)
        if b:
            carry(b - 1)
    carry(steps - 1)
    lse = jnp.concatenate([held[:, tile(t)] for t in range(cells // LANES)], axis=0)
    lse_own[...] = lse
    for k in range(n):
        lse_out[k, :, 0, :] = lse


def moment_kernel(n, blocks, parts, lse_own, carried, sg, f_out, moment_out):
    f = LOG2E * pick(sg, ROW_LOGW, blocks) - combine(parts[:, :, 0, :])
    f_out[...] = f
    weight = jnp.exp2(f + lse_own[...])
    left = [sg[t, ROW_RIGHT:PACK, :] * weight[t : t + 1] for t in range(blocks)]
    hi, low = split(jnp.concatenate(left, axis=1))
    ch, cl = split(carried[...])
    fill = jnp.zeros((LANES - RIGHT, ch.shape[1]), bf16)
    ch, cl = jnp.concatenate([ch, fill], axis=0), jnp.concatenate([cl, fill], axis=0)
    x = dot_nt(hi, ch) + dot_nt(low, ch) + dot_nt(hi, cl)
    packed = x[0:12] + pltpu.roll(x[12:24], MOMENT, 1) + pltpu.roll(x[24:36], 2 * MOMENT, 1)
    for k in range(n):
        moment_out[k, :, 0, :] = packed


def sum_kernel(n, parts, out):
    total = jnp.sum(parts[...], axis=0)
    for k in range(n):
        out[k] = total


def unpack_moment(packed):
    first = pltpu.roll(packed, LATENT, 1)
    second = pltpu.roll(packed, LANES + LATENT - MOMENT, 1)
    third = pltpu.roll(packed, LANES + LATENT - 2 * MOMENT, 1)
    x = jnp.concatenate([first, second, third, jnp.zeros((MOMENT - 36, LANES), f32)], axis=0)
    rows, lanes = iota(x.shape, 0), iota(x.shape, 1)
    x = jnp.where((rows < RANK) & (lanes >= LATENT) & (lanes < LATENT + RANK), x, 0.0)
    return jnp.concatenate([jnp.zeros((LATENT, LANES), f32), x, jnp.zeros((LANES - LATENT - MOMENT, LANES), f32)], axis=0)


def first_g_kernel(blocks, parts, f, xh, xl, rc, out, own, lc, lt, *scratch):
    moment = unpack_moment(jnp.sum(parts[...], axis=0)[:, 0, :])
    lh, ll = left_operand(xh[...], xl[...], moment)
    lt[0:FEAT, :] = lh
    lt[FEAT : 2 * FEAT, :] = lh
    lt[2 * FEAT : BIAS, :] = ll
    put_bias(lt, f[...])

    def transpose(t):
        if t < blocks:
            more = shifted(f[t : t + 1, :] + HEADROOM)
            transpose_into(lc, t, jnp.concatenate([lt[0:BIAS, tile(t)], more], axis=0))

    for t in range(rc.shape[0] // LANES, blocks):
        transpose(t)
    lse_rows(transpose, rc, lt, out, own, *scratch)


def updated(blocks, parts, gathered):
    return LOG2E * pick(gathered, ROW_LOGW, blocks) - combine(parts[:, :, 0, :])


def potential(blocks, x, gathered):
    return x * (1.0 / SCALE) + jnp.concatenate([half_square(gathered[t]) for t in range(blocks)], axis=0)


def first_f_kernel(blocks, parts, gathered, f, last, stream, fixed_in, other_in, out, fixed, other, *scratch):
    put_bias(fixed, updated(blocks, parts, gathered), {3: 1.0, 4: 1.0, 5: 1.0})

    def renew(t):
        if t < blocks:
            restream(other, t, fixed, -last[t : t + 1, :])

    for t in range(stream.shape[0] // LANES, blocks):
        renew(t)
    shifted_lse_rows(renew, stream, fixed, f[...] + HEADROOM, *scratch, out)


def second_g_kernel(blocks, parts, gathered, last, stream, fixed_in, out, fixed, *scratch):
    put_bias(fixed, updated(blocks, parts, gathered), {3: 1.0, 4: 1.0, 5: 1.0})
    shifted_lse_rows(nothing, stream, fixed, -last[...], *scratch, out)


def second_f_kernel(blocks, parts, gathered, f, stream, fixed_in, out, x_out, fixed, *scratch):
    x = updated(blocks, parts, gathered)
    x_out[...] = x
    put_bias(fixed, x, {3: 1.0, 4: 1.0, 5: 1.0})
    shifted_lse_rows(nothing, stream, fixed, f[...] + HEADROOM, *scratch, out)


def last_kernel(source_blocks, target_blocks, parts, sg, x, tg, f_out, g_out):
    f_out[...] = potential(source_blocks, updated(source_blocks, parts, sg), sg)
    g_out[...] = potential(target_blocks, x[...], tg)


def call(kernel, out, scratch=(), name=None, aliases={}, space=pltpu.VMEM, semaphores=[], vmem=32):
    spec = pl.BlockSpec(memory_space=pltpu.VMEM)
    return lambda *args: pl.pallas_call(
        kernel,
        out_shape=[jax.ShapeDtypeStruct(s, d) for s, d in out],
        in_specs=[pl.BlockSpec(memory_space=space)] * len(args),
        out_specs=[spec] * len(out),
        scratch_shapes=[pltpu.VMEM(s, d) for s, d in scratch] + semaphores,
        input_output_aliases=aliases,
        compiler_params=pltpu.CompilerParams(vmem_limit_bytes=vmem * 1024 * 1024),
        name=name,
    )(*args)


def swap(x, axis):
    return lax.all_to_all(x, axis, 0, 0)


def shards(n_src, n_tgt, *args):
    (u, a1, b1, la, v, a2, b2, lb, g, old_moment) = args
    v = v.reshape(v.shape[2:])
    a2, b2 = (x.transpose(3, 0, 1, 2).reshape(x.shape[3], 1, -1) for x in (a2, b2))
    flat = lambda x: x.reshape(1, -1)
    cells = (u.T, a1.T, b1.T, flat(la), v.T, a2, b2, flat(lb), flat(g))
    source, target = call(
        functools.partial(pack_kernel, n_tgt),
        [((n_tgt, PACK, LANES), f32), ((PACK, LANES), f32)],
        [(x.shape, f32) for x in cells],
        name="pack",
        space=pltpu.HBM,
        semaphores=[pltpu.SemaphoreType.DMA((len(cells),))],
        vmem=63,
    )(*cells)
    sg = swap(source, "tgt")
    tg = lax.all_gather(target, "src", axis=0)
    bs, bt = n_tgt, n_src
    rows, cols = bs * LANES, bt * LANES

    lse, own, carried, xh, xl, rt, rc = call(
        functools.partial(old_kernel, n_tgt, bs),
        [
            ((n_tgt, bs, 1, LANES), f32),
            ((bs, LANES), f32),
            ((RIGHT, rows), f32),
            ((FEAT, rows), bf16),
            ((FEAT, rows), bf16),
            ((DEPTH, cols), bf16),
            ((cols, DEPTH), bf16),
        ],
        [
            ((DEPTH, rows), bf16),
            ((2 * RIGHT, cols), bf16),
            ((cols, CHUNK), f32),
            ((cols, CHUNK), f32),
            ((cols, CHUNK), bf16),
            ((cols, CHUNK), bf16),
            ((cols, CHUNK), bf16),
            ((cols, CHUNK), bf16),
            ((1, rows), f32),
            ((LANES, LANES), f32),
        ],
        name="old_plan",
    )(sg, tg, old_moment)
    f, moment = call(
        functools.partial(moment_kernel, n_tgt, bs),
        [((bs, LANES), f32), ((n_tgt, 12, 1, LANES), f32)],
        name="moment",
    )(swap(lse, "tgt"), own, carried, sg)
    (moment,) = call(functools.partial(sum_kernel, n_src), [((n_src, 12, 1, LANES), f32)], name="moment_sum")(
        swap(moment, "tgt")
    )
    pipe = lambda cells, b: [((CHUNK, cells), f32)] * 2 + [((b, LANES), f32)] * 2
    part, last_g, lc, lt = call(
        functools.partial(first_g_kernel, bs),
        [((n_src, bt, 1, LANES), f32), ((bt, LANES), f32), ((rows, DEPTH), bf16), ((DEPTH, rows), bf16)],
        pipe(rows, bt),
        name="first_g",
    )(swap(moment, "src"), f, xh, xl, rc)
    fixed_t, fixed_s, stream_t = ((DEPTH, cols), bf16), ((DEPTH, rows), bf16), ((cols, DEPTH), bf16)
    part, rt, rc = call(
        functools.partial(first_f_kernel, bt),
        [((n_tgt, bs, 1, LANES), f32), fixed_t, stream_t],
        pipe(cols, bs),
        name="first_f",
        aliases={5: 1, 6: 2},
    )(swap(part, "src"), tg, f, last_g, lc, rt, rc)
    part, _ = call(
        functools.partial(second_g_kernel, bs),
        [((n_src, bt, 1, LANES), f32), fixed_s],
        pipe(rows, bt),
        name="second_g",
        aliases={4: 1},
    )(swap(part, "tgt"), sg, last_g, rc, lt)
    part, x, _ = call(
        functools.partial(second_f_kernel, bt),
        [((n_tgt, bs, 1, LANES), f32), ((bt, LANES), f32), fixed_t],
        pipe(cols, bs),
        name="second_f",
        aliases={4: 2},
    )(swap(part, "src"), tg, f, lc, rt)
    f, g = call(
        functools.partial(last_kernel, bs, bt),
        [((bs, LANES), f32), ((bt, LANES), f32)],
        name="last",
    )(swap(part, "tgt"), sg, x, tg)
    return f.reshape(-1), g.reshape(-1)


def solution(mesh):
    return jax.shard_map(
        functools.partial(shards, mesh.shape["src"], mesh.shape["tgt"]),
        mesh=mesh,
        in_specs=(
            P(("src", "tgt"), None),
            P(("src", "tgt"), None),
            P(("src", "tgt"), None),
            P(("src", "tgt")),
            P("tgt", "src", None, None),
            P("tgt", "src", None, None),
            P("tgt", "src", None, None),
            P("tgt", "src", None),
            P("tgt", "src", None),
            P(),
        ),
        out_specs=(P("src"), P("tgt")),
        check_vma=False,
    )
```
